256 devices in a mesh: veh: 32 (over z, x), req: 8 (over y, core).
Axes of the slice: x: 4, y: 4, z: 8, core: 2. Of those that a mesh axis runs over, the one named last changes fastest.
Arguments:
- vehicle_emb: bfloat16 [32768, 128], P(('veh', 'req')), may hold values from -40 to 40
- request_emb: bfloat16 [32768, 128], P('req'), may hold values from -8 to 8
- request_feat: bfloat16 [32768, 256], P('req'), may hold values from -6 to 6
- log_supply: float32 [32768], P('veh'), may hold values from -1.2 to 1.2
- log_demand: float32 [32768], P('req'), may hold values from -1.2 to 1.2
Outputs:
- assigned: float32 [32768, 256], P(('veh', 'req'))
The draws below stay inside these ranges and needn't reach their ends.
All inputs are finite; a program needn't handle non-finite values.
Results may differ from the reference program's by a relative error of at most 0.0017.
Values may be sent and summed in bfloat16 or wider, within the bound.
A program may use at most 64 MiB of HBM per device.

```python
import math
import jax
import jax.numpy as jnp
from jax import lax

E = 128
F = 256
REQ_DEV = 4096
VEHICLES = 32768
REQUESTS = 32768
N_REQ = 8


def shared_embeddings(key):
    base_key = jax.random.fold_in(key, 11)
    key_req, key_veh = jax.random.split(base_key, 2)
    requests = jax.random.normal(key_req, (REQUESTS, E), jnp.float32)
    vehicles = jax.random.normal(key_veh, (VEHICLES, E), jnp.float32)
    return (jnp.clip(vehicles, -40.0, 40.0), jnp.clip(requests, -8.0, 8.0))


def draw_vehicle_emb(key, part):
    return shared_embeddings(key)[0].astype(jnp.bfloat16)


def draw_request_emb(key, part):
    return shared_embeddings(key)[1].astype(jnp.bfloat16)


def steps_of(own_key, shape, shards, smallest, top_value):
    loudness = 1.0
    for dim, parts in shards:
        draws = jax.random.uniform(jax.random.fold_in(jax.random.fold_in(own_key, 6), dim), (parts,), jnp.float32, smallest / len(shards), top_value / len(shards))
        loudness = loudness * jnp.repeat(jnp.exp(draws), shape[dim] // parts).reshape((-1,) + (1,) * (len(shape) - 1 - dim))
    return loudness


def scatter_about(key, dims, spread, bound, pieces=(), kind=jnp.bfloat16):
    factor_of = steps_of(key, dims, pieces, -0.22, 0.18) if pieces else 1.0
    values = jax.random.normal(key, dims, jnp.float32) * spread * factor_of
    return jnp.minimum(jnp.maximum(values, -bound), bound).astype(kind)


def setup_inputs(seed: int = 0) -> dict:
    streams_of = jax.random.split(jax.random.key(seed), 6)
    vehicle_emb = draw_vehicle_emb(jax.random.fold_in(streams_of[5], 71), 0)
    request_emb = draw_request_emb(jax.random.fold_in(streams_of[5], 71), 0)
    request_feat = scatter_about(streams_of[2], (REQUESTS, F), 1.0, 6.0, ((0, 8),))
    log_supply = jnp.clip(jax.random.uniform(streams_of[3], (VEHICLES,), jnp.float32, -1.2, 1.2) * steps_of(streams_of[3], (VEHICLES,), ((0, 32),), -0.4, 0.0), -1.2, 1.2)
    log_demand = jnp.clip(jax.random.uniform(streams_of[4], (REQUESTS,), jnp.float32, -1.2, 1.2) * steps_of(streams_of[4], (REQUESTS,), ((0, 8),), -0.4, 0.0), -1.2, 1.2)
    return dict(vehicle_emb=vehicle_emb, request_emb=request_emb, request_feat=request_feat, log_supply=log_supply, log_demand=log_demand)


def block_scores(vehicle_block, request_emb):
    score_scale = 3.0 / math.sqrt(E)
    return lax.dot_general(vehicle_block, request_emb, (((1,), (1,)), ((), ())), preferred_element_type=jnp.float32) * score_scale

def reference(vehicle_emb, request_emb, request_feat, log_supply, log_demand):
    block_rows = min(1024, VEHICLES)
    block_count = VEHICLES // block_rows
    vehicle_blocks = vehicle_emb.reshape(block_count, block_rows, E)

    def column_lse(shift):
        shift_blocks = shift.reshape(block_count, block_rows)

        def column_step(state_pair, element):
            running, accrued = state_pair
            vehicle_block, shift_block = element
            logits = block_scores(vehicle_block, request_emb) + shift_block[:, None]
            highest = jnp.maximum(running, lax.optimization_barrier(jnp.max(logits, axis=0)))
            accrued = accrued * jnp.exp(running - highest) + lax.optimization_barrier(jnp.sum(jnp.exp(logits - highest[None, :]), axis=0))
            return ((highest, accrued), None)
        start_pair = (jnp.full((REQUESTS,), -1e+30, jnp.float32), jnp.zeros((REQUESTS,), jnp.float32))
        (highest, accrued), unused = lax.scan(column_step, start_pair, (vehicle_blocks, shift_blocks))
        return highest + jnp.log(accrued)

    def row_lse(potential):

        def row_block(vehicle_block):
            logits = block_scores(vehicle_block, request_emb) + potential[None, :]
            highest = lax.optimization_barrier(jnp.max(logits, axis=1))
            return highest + jnp.log(lax.optimization_barrier(jnp.sum(jnp.exp(logits - highest[:, None]), axis=1)))
        return lax.map(row_block, vehicle_blocks).reshape(VEHICLES)
    demand_first = log_demand - column_lse(jnp.zeros((VEHICLES,), jnp.float32))
    supply_pot = log_supply - row_lse(demand_first)
    demand_second = log_demand - column_lse(supply_pot)
    feat_blocks = request_feat.astype(jnp.float32).reshape(N_REQ, REQ_DEV, F)

    def assign_block(vehicle_block):
        logits = block_scores(vehicle_block, request_emb) + demand_second[None, :]
        logits = logits.reshape(block_rows, N_REQ, REQ_DEV)
        block_peak = lax.optimization_barrier(jnp.max(logits, axis=2))
        powers = jnp.exp(logits - block_peak[:, :, None])
        block_mass = lax.optimization_barrier(jnp.sum(powers, axis=2))
        weights = lax.optimization_barrier(powers.astype(jnp.bfloat16)).astype(jnp.float32)
        block_feat = jnp.einsum('bnr,nrf->bnf', weights, feat_blocks, precision=lax.Precision.HIGHEST)
        row_top = lax.optimization_barrier(jnp.max(block_peak, axis=1))
        factor = jnp.exp(block_peak - row_top[:, None])
        numerator = lax.optimization_barrier(jnp.sum(block_feat * factor[:, :, None], axis=1))
        denominator = lax.optimization_barrier(jnp.sum(block_mass * factor, axis=1))
        return numerator / denominator[:, None]
    return lax.map(assign_block, vehicle_blocks).reshape(VEHICLES, F)
```

```python
import functools
import math

import jax
import jax.numpy as jnp
from jax import lax
from jax.experimental import pallas as pl
from jax.experimental.pallas import tpu as pltpu
from jax.sharding import PartitionSpec as P

MESH = pl.DeviceIdType.MESH
LOG2E = 1.4426950408889634
NX, NZ, NY = 4, 8, 4
NB = 8
BLK = 128
LANES = 128
NCHUNK = 4
TINY = 1e-30


def score_rows(v_all, r_t, z, top, slot, scale):
    width = 512
    v = v_all[slot]
    rows = pl.ds(pl.multiple_of(slot * BLK, BLK), BLK)

    def step(t, _):
        cols = pl.ds(pl.multiple_of(t * width, width), width)
        s = lax.dot_general(v, r_t[:, cols], (((1,), (0,)), ((), ())), preferred_element_type=jnp.float32) * scale
        z[rows, cols] = s
        top[:, cols] = jnp.maximum(top[:, cols], jnp.max(s.reshape(BLK // 8, 8, width), axis=0))
        return 0

    lax.fori_loop(0, z.shape[1] // width, step, 0)


def column_lse(z, top, c, cw):
    cols = pl.ds(c * cw, cw)
    peak = jnp.max(top[:, cols], axis=0, keepdims=True)
    rows = 32

    def step(t, acc):
        e = jnp.exp2(z[pl.ds(pl.multiple_of(t * rows, rows), rows), cols] - peak)
        return acc + jnp.sum(e.reshape(rows // 8, 8, cw), axis=0)

    acc = lax.fori_loop(0, z.shape[0] // rows, step, jnp.zeros((8, cw), jnp.float32), unroll=2)
    return peak + jnp.log(jnp.sum(acc, axis=0, keepdims=True)) * LOG2E


def row_pass(z, d, m, s, c, cw):
    rows = 16
    kk = cw // LANES

    def step(t, _):
        rr = pl.ds(pl.multiple_of(t * rows, rows), rows)
        ys = [z[rr, pl.ds(c * cw + k * LANES, LANES)] + d[:, pl.ds(c * cw + k * LANES, LANES)] for k in range(kk)]
        peak = functools.reduce(jnp.maximum, ys)
        total = None
        for k in range(kk):
            e = jnp.exp2(ys[k] - peak)
            z[rr, pl.ds(c * cw + k * LANES, LANES)] = e
            total = e if total is None else total + e
        m[c, rr, :] = peak
        s[c, rr, :] = total
        return 0

    lax.fori_loop(0, z.shape[0] // rows, step, 0, unroll=2)


def row_totals(m, s, out):
    def step(g, _):
        rr = pl.ds(pl.multiple_of(g * BLK, BLK), BLK)
        peak = functools.reduce(jnp.maximum, [m[c, rr, :] for c in range(NCHUNK)])
        total = sum(s[c, rr, :] * jnp.exp2(m[c, rr, :] - peak) for c in range(NCHUNK))
        pt, tt = peak.T, total.T
        top = jnp.max(pt, axis=0, keepdims=True)
        out[g] = top + jnp.log(jnp.sum(tt * jnp.exp2(pt - top), axis=0, keepdims=True)) * LOG2E
        return 0

    lax.fori_loop(0, NB, step, 0)


def row_scales(m, sp):
    def step(g, _):
        rr = pl.ds(pl.multiple_of(g * BLK, BLK), BLK)
        col = jnp.broadcast_to(sp[g], (BLK, LANES)).T
        for c in range(NCHUNK):
            m[c, rr, :] = jnp.exp2(m[c, rr, :] + col)
        return 0

    lax.fori_loop(0, NB, step, 0)


def column_sum(z, u, c, cw):
    rows = 32
    kk = cw // LANES

    def step(t, accs):
        rr = pl.ds(pl.multiple_of(t * rows, rows), rows)
        ut = u[c, rr, :]
        return tuple(
            a + jnp.sum((z[rr, pl.ds(c * cw + k * LANES, LANES)] * ut).reshape(rows // 8, 8, LANES), axis=0)
            for k, a in enumerate(accs)
        )

    zero = tuple(jnp.zeros((8, LANES), jnp.float32) for _ in range(kk))
    accs = lax.fori_loop(0, z.shape[0] // rows, step, zero, unroll=2)
    return jnp.concatenate([jnp.sum(a, axis=0, keepdims=True) for a in accs], axis=1)


def weight_pass(z, u, gain, tm, ms, c, cw):
    rows = 16
    kk = cw // LANES

    def step(t, _):
        rr = pl.ds(pl.multiple_of(t * rows, rows), rows)
        ut = u[c, rr, :]
        peak = total = None
        for k in range(kk):
            cols = pl.ds(c * cw + k * LANES, LANES)
            e = z[rr, cols] * ut * gain[:, cols]
            z[rr, cols] = e
            peak = e if peak is None else jnp.maximum(peak, e)
            total = e if total is None else total + e
        if c > 0:
            peak, total = jnp.maximum(peak, tm[rr, :]), total + ms[rr, :]
        tm[rr, :] = peak
        ms[rr, :] = total
        return 0

    lax.fori_loop(0, z.shape[0] // rows, step, 0, unroll=2)


def block_features(z, tm, feat, row0, rows):
    rr = pl.ds(pl.multiple_of(row0, rows), rows)
    peak = jnp.maximum(jnp.max(tm[rr, :], axis=1, keepdims=True), TINY)
    w = (z[rr, :] * (1.0 / peak)).astype(jnp.bfloat16)
    return jnp.dot(w, feat[...], preferred_element_type=jnp.float32) * peak


def lse_parts(parts):
    top = jnp.max(parts, axis=0)
    return top + jnp.log(jnp.sum(jnp.exp2(parts - top[None]), axis=0)) * LOG2E


def kernel(v_hbm, r_hbm, feat_hbm, sup_hbm, dem_hbm, out,
           v_all, r, r_t, feat, sup, dem, z, top, d, gain, m, s, tm, ms,
           xbuf, zbuf, rowbuf, massown, massbuf, sp, fpart, fmate, fsend, frecv,
           load_sem, ag_send, ag_recv, x_send, x_recv, z_send, z_recv, row_sem, mass_sem,
           mate_send, mate_recv, f_send, f_recv):
    me, b = lax.axis_index("veh"), lax.axis_index("req")
    zc, xc = me // NX, lax.rem(me, NX)
    y, core = b // 2, lax.rem(b, 2)
    cw = z.shape[1] // NCHUNK
    scale = 3.0 / math.sqrt(v_hbm.shape[1]) * LOG2E

    def x_peer(k):
        return (zc * NX + lax.rem(xc + k, NX), b)

    def z_peer(k):
        return (lax.rem(zc + k, NZ) * NX + xc, b)

    def req_peer(k):
        return (me, lax.rem(b + k, NB))

    loads = [
        pltpu.make_async_copy(v_hbm, v_all.at[b], load_sem.at[0]),
        pltpu.make_async_copy(r_hbm, r, load_sem.at[1]),
        pltpu.make_async_copy(sup_hbm, sup, load_sem.at[2]),
        pltpu.make_async_copy(dem_hbm, dem, load_sem.at[3]),
        pltpu.make_async_copy(feat_hbm, feat, load_sem.at[4]),
    ]
    for load in loads:
        load.start()
    barrier = pltpu.get_barrier_semaphore()
    for k in range(1, NX):
        pl.semaphore_signal(barrier, inc=1, device_id=x_peer(k), device_id_type=MESH)
    for k in range(1, NZ):
        pl.semaphore_signal(barrier, inc=1, device_id=z_peer(k), device_id_type=MESH)
    for k in range(1, NB):
        pl.semaphore_signal(barrier, inc=1, device_id=req_peer(k), device_id_type=MESH)
    top[...] = jnp.full(top.shape, -3e38, jnp.float32)
    loads[1].wait()

    def flip(t, _):
        w = 512
        r_t[:, pl.ds(pl.multiple_of(t * w, w), w)] = r[pl.ds(pl.multiple_of(t * w, w), w), :].T
        return 0

    lax.fori_loop(0, r.shape[0] // 512, flip, 0)
    loads[0].wait()
    pl.semaphore_wait(barrier, NX + NZ + NB - 3)

    order = (1, 2, 6, 7, 3, 5, 4)
    gathers = []
    for k in order:
        copy = pltpu.make_async_remote_copy(
            v_all.at[b], v_all.at[b], ag_send.at[k], ag_recv.at[NB - k], device_id=req_peer(k), device_id_type=MESH)
        copy.start()
        gathers.append(copy)
    score_rows(v_all, r_t, z, top, b, scale)
    for k in order:
        slot = lax.rem(b + k, NB)
        pltpu.make_async_copy(v_all.at[slot], v_all.at[slot], ag_recv.at[k]).wait()
        score_rows(v_all, r_t, z, top, slot, scale)

    def x_start(a, c):
        for k in range(1, NX):
            pltpu.make_async_remote_copy(
                xbuf.at[a, c, NX - 1], xbuf.at[a, c, NX - 1 - k], x_send.at[a, c], x_recv.at[a, c],
                device_id=x_peer(k), device_id_type=MESH).start()

    def z_start(a, c):
        for k in range(1, NZ):
            pltpu.make_async_remote_copy(
                zbuf.at[a, c, NZ - 1], zbuf.at[a, c, NZ - 1 - k], z_send.at[a, c], z_recv.at[a, c],
                device_id=z_peer(k), device_id_type=MESH).start()

    def all_of(buf, n, sem):
        pltpu.make_async_copy(buf.at[pl.ds(0, n)], buf.at[pl.ds(0, n)], sem).wait()

    loads[2].wait()
    loads[3].wait()
    for c in range(NCHUNK):
        xbuf[0, c, NX - 1] = column_lse(z, top, c, cw)
        x_start(0, c)
    for c in range(NCHUNK):
        all_of(xbuf.at[0, c], NX - 1, x_recv.at[0, c])
        zbuf[0, c, NZ - 1] = lse_parts(xbuf[0, c])
        z_start(0, c)
    for c in range(NCHUNK):
        all_of(zbuf.at[0, c], NZ - 1, z_recv.at[0, c])
        cols = pl.ds(c * cw, cw)
        d[:, cols] = dem[:, cols] * LOG2E - lse_parts(zbuf[0, c])
        row_pass(z, d, m, s, c, cw)

    row_totals(m, s, rowbuf.at[NB - 1])
    for k in range(1, NB):
        pltpu.make_async_remote_copy(
            rowbuf.at[NB - 1], rowbuf.at[NB - 1 - k], row_sem.at[0], row_sem.at[1],
            device_id=req_peer(k), device_id_type=MESH).start()
    all_of(rowbuf, NB - 1, row_sem.at[1])
    sp[...] = sup[...] * LOG2E - lse_parts(rowbuf[...])
    row_scales(m, sp)

    for c in range(NCHUNK):
        xbuf[1, c, NX - 1] = column_sum(z, m, c, cw)
        x_start(1, c)
    for c in range(NCHUNK):
        all_of(xbuf.at[1, c], NX - 1, x_recv.at[1, c])
        zbuf[1, c, NZ - 1] = jnp.sum(xbuf[1, c], axis=0)
        z_start(1, c)
    for c in range(NCHUNK):
        all_of(zbuf.at[1, c], NZ - 1, z_recv.at[1, c])
        cols = pl.ds(c * cw, cw)
        gain[:, cols] = jnp.exp2(dem[:, cols] * LOG2E) / jnp.sum(zbuf[1, c], axis=0)
        weight_pass(z, m, gain, tm, ms, c, cw)

    def mass_step(g, _):
        rr = pl.ds(pl.multiple_of(g * BLK, BLK), BLK)
        massown[g] = jnp.sum(ms[rr, :].T, axis=0, keepdims=True)
        return 0

    lax.fori_loop(0, NB, mass_step, 0)
    for k in range(1, NB):
        pltpu.make_async_remote_copy(
            massown.at[lax.rem(b + k, NB)], massbuf.at[NB - 1 - k], mass_sem.at[0], mass_sem.at[1],
            device_id=req_peer(k), device_id_type=MESH).start()
    massbuf[NB - 1] = massown[b]

    loads[4].wait()
    steps = (2, 1, 3, 0)

    def mate_copy(i):
        return pltpu.make_async_remote_copy(
            fpart.at[i, 1 - core], fmate.at[i], mate_send.at[i], mate_recv.at[i],
            device_id=(me, y * 2 + 1 - core), device_id_type=MESH)

    def out_copy(i):
        return pltpu.make_async_remote_copy(
            fsend.at[i], frecv.at[i], f_send.at[i], f_recv.at[i],
            device_id=(me, lax.rem(y + steps[i], NY) * 2 + core), device_id_type=MESH)

    def pass_on(i):
        mate_copy(i).wait_recv()
        fsend[i] = (fpart[i, core] + fmate[i]).astype(jnp.bfloat16)
        out_copy(i).start()

    for i, step in enumerate(steps):
        row0 = lax.rem(y + step, NY) * 2 * BLK
        fpart[i] = block_features(z, tm, feat, row0, 2 * BLK).reshape(2, BLK, feat.shape[1])
        mate_copy(i).start()
        if i > 0:
            pass_on(i - 1)
    all_of(massbuf, NB - 1, mass_sem.at[1])
    mass = jnp.sum(massbuf[...], axis=0)
    inv = 1.0 / jnp.broadcast_to(mass, (BLK, LANES)).T
    last = len(steps) - 1
    mate_copy(last).wait_recv()
    total = fpart[last, core] + fmate[last]
    for i in range(last):
        out_copy(i).wait_recv()
        total = total + frecv[i].astype(jnp.float32)
    for k in range(feat.shape[1] // LANES):
        out[:, k * LANES:(k + 1) * LANES] = total[:, k * LANES:(k + 1) * LANES] * inv

    for copy in gathers:
        copy.wait_send()
    for a in range(2):
        for c in range(NCHUNK):
            all_of(xbuf.at[a, c], NX - 1, x_send.at[a, c])
            all_of(zbuf.at[a, c], NZ - 1, z_send.at[a, c])
    all_of(rowbuf, NB - 1, row_sem.at[0])
    all_of(massbuf, NB - 1, mass_sem.at[0])
    for i in range(len(steps)):
        mate_copy(i).wait_send()
    for i in range(last):
        out_copy(i).wait_send()


def local(vehicle_emb, request_emb, request_feat, log_supply, log_demand):
    rows, cols, width = BLK * NB, request_emb.shape[0], request_feat.shape[1]
    cw = cols // NCHUNK
    f32, bf16 = jnp.float32, jnp.bfloat16
    dma = pltpu.SemaphoreType.DMA
    scratch = [
        pltpu.VMEM((NB, BLK, vehicle_emb.shape[1]), bf16),
        pltpu.VMEM(request_emb.shape, bf16),
        pltpu.VMEM(request_emb.shape[::-1], bf16),
        pltpu.VMEM(request_feat.shape, bf16),
        pltpu.VMEM((NB, 1, LANES), f32),
        pltpu.VMEM((1, cols), f32),
        pltpu.VMEM((rows, cols), f32),
        pltpu.VMEM((8, cols), f32),
        pltpu.VMEM((1, cols), f32),
        pltpu.VMEM((1, cols), f32),
        pltpu.VMEM((NCHUNK, rows, LANES), f32),
        pltpu.VMEM((NCHUNK, rows, LANES), f32),
        pltpu.VMEM((rows, LANES), f32),
        pltpu.VMEM((rows, LANES), f32),
        pltpu.VMEM((2, NCHUNK, NX, 1, cw), f32),
        pltpu.VMEM((2, NCHUNK, NZ, 1, cw), f32),
        pltpu.VMEM((NB, NB, 1, LANES), f32),
        pltpu.VMEM((NB, 1, LANES), f32),
        pltpu.VMEM((NB, 1, LANES), f32),
        pltpu.VMEM((NB, 1, LANES), f32),
        pltpu.VMEM((NY, 2, BLK, width), f32),
        pltpu.VMEM((NY, BLK, width), f32),
        pltpu.VMEM((NY - 1, BLK, width), bf16),
        pltpu.VMEM((NY - 1, BLK, width), bf16),
        dma((5,)), dma((NB,)), dma((NB,)),
        dma((2, NCHUNK)), dma((2, NCHUNK)), dma((2, NCHUNK)), dma((2, NCHUNK)),
        dma((2,)), dma((2,)),
        dma((NY,)), dma((NY,)), dma((NY - 1,)), dma((NY - 1,)),
    ]
    return pl.pallas_call(
        kernel,
        out_shape=jax.ShapeDtypeStruct((BLK, width), f32),
        in_specs=[pl.BlockSpec(memory_space=pl.ANY)] * 5,
        out_specs=pl.BlockSpec(memory_space=pltpu.VMEM),
        scratch_shapes=scratch,
        compiler_params=pltpu.CompilerParams(
            collective_id=0, has_side_effects=True, vmem_limit_bytes=56 * 2**20),
        cost_estimate=pl.CostEstimate(
            flops=2 * rows * cols * (vehicle_emb.shape[1] + width), bytes_accessed=4 * 2**20,
            transcendentals=2 * rows * cols),
        name="sinkhorn_assign",
    )(vehicle_emb, request_emb, request_feat, log_supply.reshape(NB, 1, LANES), log_demand.reshape(1, cols))


def solution(mesh):
    in_specs = (P(("veh", "req"), None), P("req", None), P("req", None), P("veh"), P("req"))
    out_specs = P(("veh", "req"), None)
    return jax.shard_map(local, mesh=mesh, in_specs=in_specs, out_specs=out_specs, check_vma=False)
```

```python
import functools
import math

import jax
import jax.numpy as jnp
from jax import lax
from jax.experimental import pallas as pl
from jax.experimental.pallas import tpu as pltpu
from jax.sharding import PartitionSpec as P

MESH = pl.DeviceIdType.MESH
LOG2E = 1.4426950408889634
NX, NZ, NY = 4, 8, 4
NB = 8
BLK = 128
LANES = 128
NCHUNK = 4
TINY = 1e-30


def score_rows(v_all, r_t, z, top, acc, slot, scale, first):
    width = 512
    v = v_all[slot]
    rows = pl.ds(pl.multiple_of(slot * BLK, BLK), BLK)
    for t in range(z.shape[1] // width):
        cols = pl.ds(t * width, width)
        s = lax.dot_general(v, r_t[:, cols], (((1,), (0,)), ((), ())), preferred_element_type=jnp.float32) * scale
        z[rows, cols] = s
        s = s.reshape(BLK // 8, 8, width)
        peak = jnp.max(s, axis=0)
        if not first:
            old = top[:, cols]
            peak = jnp.maximum(old, peak)
        e = jnp.sum(jnp.exp2(s - peak[None]), axis=0)
        top[:, cols] = peak
        acc[:, cols] = e if first else acc[:, cols] * jnp.exp2(old - peak) + e


def column_lse(top, acc):
    t = top[...]
    peak = jnp.max(t, axis=0, keepdims=True)
    return peak + jnp.log(jnp.sum(acc[...] * jnp.exp2(t - peak), axis=0, keepdims=True)) * LOG2E


def row_pass(z, d, w, m, s, c, cw):
    rows = 32
    kk = cw // LANES

    def step(t, _):
        rr = pl.ds(pl.multiple_of(t * rows, rows), rows)
        ys = [z[rr, pl.ds(c * cw + k * LANES, LANES)] + d[:, pl.ds(c * cw + k * LANES, LANES)] for k in range(kk)]
        peak = functools.reduce(jnp.maximum, ys)
        total = None
        for k in range(kk):
            e = jnp.exp2(ys[k] - peak)
            w[rr, pl.ds(c * cw + k * LANES, LANES)] = e
            total = e if total is None else total + e
        m[c, rr, :] = peak
        s[c, rr, :] = total
        return 0

    lax.fori_loop(0, z.shape[0] // rows, step, 0, unroll=2)


def row_totals(m, s, out):
    for g in range(NB):
        rr = pl.ds(g * BLK, BLK)
        peak = functools.reduce(jnp.maximum, [m[c, rr, :] for c in range(NCHUNK)])
        total = sum(s[c, rr, :] * jnp.exp2(m[c, rr, :] - peak) for c in range(NCHUNK))
        pt, tt = peak.T, total.T
        top = jnp.max(pt, axis=0, keepdims=True)
        out[g] = top + jnp.log(jnp.sum(tt * jnp.exp2(pt - top), axis=0, keepdims=True)) * LOG2E


def row_scales(m, sp):
    for g in range(NB):
        rr = pl.ds(g * BLK, BLK)
        col = jnp.broadcast_to(sp[g], (BLK, LANES)).T
        for c in range(NCHUNK):
            m[c, rr, :] = jnp.exp2(m[c, rr, :] + col)


def column_sum(w, u, c, cw):
    rows = 32
    kk = cw // LANES

    def step(t, accs):
        rr = pl.ds(pl.multiple_of(t * rows, rows), rows)
        ut = u[c, rr, :]
        return tuple(
            a + jnp.sum((w[rr, pl.ds(c * cw + k * LANES, LANES)] * ut).reshape(rows // 8, 8, LANES), axis=0)
            for k, a in enumerate(accs)
        )

    zero = tuple(jnp.zeros((8, LANES), jnp.float32) for _ in range(kk))
    accs = lax.fori_loop(0, w.shape[0] // rows, step, zero, unroll=4)
    return jnp.concatenate([jnp.sum(a, axis=0, keepdims=True) for a in accs], axis=1)


def weight_pass(w, u, gain, t, tm, ms, c, cw):
    rows = 64
    kk = cw // LANES

    def step(i, _):
        rr = pl.ds(pl.multiple_of(i * rows, rows), rows)
        ut = u[c, rr, :]
        peak = total = None
        for k in range(kk):
            cols = pl.ds(c * cw + k * LANES, LANES)
            e = w[rr, cols] * ut * gain[:, cols]
            t[rr, cols] = e
            peak = e if peak is None else jnp.maximum(peak, e)
            total = e if total is None else total + e
        if c > 0:
            peak, total = jnp.maximum(peak, tm[rr, :]), total + ms[rr, :]
        tm[rr, :] = peak
        ms[rr, :] = total
        return 0

    lax.fori_loop(0, w.shape[0] // rows, step, 0)


def block_features(t, tm, feat, row0, rows):
    rr = pl.ds(pl.multiple_of(row0, rows), rows)
    peak = jnp.maximum(jnp.max(tm[rr, :], axis=1, keepdims=True), TINY)
    weights = (t[rr, :] * (1.0 / peak)).astype(jnp.bfloat16)
    return jnp.dot(weights, feat[...], preferred_element_type=jnp.float32) * peak


def lse_parts(parts):
    top = jnp.max(parts, axis=0)
    return top + jnp.log(jnp.sum(jnp.exp2(parts - top[None]), axis=0)) * LOG2E


def kernel(v_hbm, r_hbm, feat_hbm, sup_hbm, dem_hbm, out,
           v_all, r, r_t, feat, sup, dem, z, w, top, acc, d, gain, m, s, tm, ms,
           xwide, xbuf, zbuf, rowbuf, massown, massbuf, sp, fpart, fmate, fsend, frecv,
           load_sem, ag_send, ag_recv, xw_sem, x_send, x_recv, z_send, z_recv, row_sem, mass_sem,
           mate_send, mate_recv, f_send, f_recv):
    me, b = lax.axis_index("veh"), lax.axis_index("req")
    zc, xc = me // NX, lax.rem(me, NX)
    y, core = b // 2, lax.rem(b, 2)
    cw = z.shape[1] // NCHUNK
    scale = 3.0 / math.sqrt(v_hbm.shape[1]) * LOG2E

    def x_peer(k):
        return (zc * NX + lax.rem(xc + k, NX), b)

    def z_peer(k):
        return (lax.rem(zc + k, NZ) * NX + xc, b)

    def req_peer(k):
        return (me, lax.rem(b + k, NB))

    loads = [
        pltpu.make_async_copy(v_hbm, v_all.at[b], load_sem.at[0]),
        pltpu.make_async_copy(r_hbm, r, load_sem.at[1]),
        pltpu.make_async_copy(sup_hbm, sup, load_sem.at[2]),
        pltpu.make_async_copy(dem_hbm, dem, load_sem.at[3]),
        pltpu.make_async_copy(feat_hbm, feat, load_sem.at[4]),
    ]
    for load in loads:
        load.start()
    barrier = pltpu.get_barrier_semaphore()
    for k in range(1, NX):
        pl.semaphore_signal(barrier, inc=1, device_id=x_peer(k), device_id_type=MESH)
    for k in range(1, NZ):
        pl.semaphore_signal(barrier, inc=1, device_id=z_peer(k), device_id_type=MESH)
    for k in range(1, NB):
        pl.semaphore_signal(barrier, inc=1, device_id=req_peer(k), device_id_type=MESH)
    loads[1].wait()

    def flip(t, _):
        part = pl.ds(pl.multiple_of(t * 512, 512), 512)
        r_t[:, part] = r[part, :].T
        return 0

    lax.fori_loop(0, r.shape[0] // 512, flip, 0)
    loads[0].wait()
    pl.semaphore_wait(barrier, NX + NZ + NB - 3)

    order = (1, 7, 2, 6, 3, 5, 4)
    gathers = []
    for k in order:
        copy = pltpu.make_async_remote_copy(
            v_all.at[b], v_all.at[b], ag_send.at[k], ag_recv.at[NB - k], device_id=req_peer(k), device_id_type=MESH)
        copy.start()
        gathers.append(copy)
    score_rows(v_all, r_t, z, top, acc, b, scale, True)
    for k in order:
        slot = lax.rem(b + k, NB)
        pltpu.make_async_copy(v_all.at[slot], v_all.at[slot], ag_recv.at[k]).wait()
        score_rows(v_all, r_t, z, top, acc, slot, scale, False)

    def x_start(c):
        for k in range(1, NX):
            pltpu.make_async_remote_copy(
                xbuf.at[c, NX - 1], xbuf.at[c, NX - 1 - k], x_send.at[c], x_recv.at[c],
                device_id=x_peer(k), device_id_type=MESH).start()

    def z_start(a, c):
        for k in range(1, NZ):
            pltpu.make_async_remote_copy(
                zbuf.at[a, c, NZ - 1], zbuf.at[a, c, NZ - 1 - k], z_send.at[a, c], z_recv.at[a, c],
                device_id=z_peer(k), device_id_type=MESH).start()

    def all_of(buf, n, sem):
        pltpu.make_async_copy(buf.at[pl.ds(0, n)], buf.at[pl.ds(0, n)], sem).wait()

    loads[2].wait()
    loads[3].wait()
    xwide[NX - 1] = column_lse(top, acc)
    for k in range(1, NX):
        pltpu.make_async_remote_copy(
            xwide.at[NX - 1], xwide.at[NX - 1 - k], xw_sem.at[0], xw_sem.at[1],
            device_id=x_peer(k), device_id_type=MESH).start()
    all_of(xwide, NX - 1, xw_sem.at[1])
    for c in range(NCHUNK):
        zbuf[0, c, NZ - 1] = lse_parts(xwide[:, :, pl.ds(c * cw, cw)])
        z_start(0, c)
    for c in range(NCHUNK):
        all_of(zbuf.at[0, c], NZ - 1, z_recv.at[0, c])
        cols = pl.ds(c * cw, cw)
        d[:, cols] = dem[:, cols] * LOG2E - lse_parts(zbuf[0, c])
        row_pass(z, d, w, m, s, c, cw)

    row_totals(m, s, rowbuf.at[NB - 1])
    for k in range(1, NB):
        pltpu.make_async_remote_copy(
            rowbuf.at[NB - 1], rowbuf.at[NB - 1 - k], row_sem.at[0], row_sem.at[1],
            device_id=req_peer(k), device_id_type=MESH).start()
    all_of(rowbuf, NB - 1, row_sem.at[1])
    sp[...] = sup[...] * LOG2E - lse_parts(rowbuf[...])
    row_scales(m, sp)

    for c in range(NCHUNK):
        xbuf[c, NX - 1] = column_sum(w, m, c, cw)
        x_start(c)
    for c in range(NCHUNK):
        all_of(xbuf.at[c], NX - 1, x_recv.at[c])
        zbuf[1, c, NZ - 1] = jnp.sum(xbuf[c], axis=0)
        z_start(1, c)
    for c in range(NCHUNK):
        all_of(zbuf.at[1, c], NZ - 1, z_recv.at[1, c])
        cols = pl.ds(c * cw, cw)
        gain[:, cols] = jnp.exp2(dem[:, cols] * LOG2E) / jnp.sum(zbuf[1, c], axis=0)
        weight_pass(w, m, gain, z, tm, ms, c, cw)

    def mass_step(g, _):
        rr = pl.ds(pl.multiple_of(g * BLK, BLK), BLK)
        massown[g] = jnp.sum(ms[rr, :].T, axis=0, keepdims=True)
        return 0

    lax.fori_loop(0, NB, mass_step, 0)
    for k in range(1, NB):
        pltpu.make_async_remote_copy(
            massown.at[lax.rem(b + k, NB)], massbuf.at[NB - 1 - k], mass_sem.at[0], mass_sem.at[1],
            device_id=req_peer(k), device_id_type=MESH).start()
    massbuf[NB - 1] = massown[b]

    loads[4].wait()
    steps = (2, 1, 3, 0)

    def mate_copy(i):
        return pltpu.make_async_remote_copy(
            fpart.at[i, 1 - core], fmate.at[i], mate_send.at[i], mate_recv.at[i],
            device_id=(me, y * 2 + 1 - core), device_id_type=MESH)

    def out_copy(i):
        return pltpu.make_async_remote_copy(
            fsend.at[i], frecv.at[i], f_send.at[i], f_recv.at[i],
            device_id=(me, lax.rem(y + steps[i], NY) * 2 + core), device_id_type=MESH)

    def pass_on(i):
        mate_copy(i).wait_recv()
        fsend[i] = (fpart[i, core] + fmate[i]).astype(jnp.bfloat16)
        out_copy(i).start()

    for i, step in enumerate(steps):
        row0 = lax.rem(y + step, NY) * 2 * BLK
        fpart[i] = block_features(z, tm, feat, row0, 2 * BLK).reshape(2, BLK, feat.shape[1])
        mate_copy(i).start()
        if i > 0:
            pass_on(i - 1)
    all_of(massbuf, NB - 1, mass_sem.at[1])
    mass = jnp.sum(massbuf[...], axis=0)
    inv = 1.0 / jnp.broadcast_to(mass, (BLK, LANES)).T
    last = len(steps) - 1
    mate_copy(last).wait_recv()
    total = fpart[last, core] + fmate[last]
    for i in range(last):
        out_copy(i).wait_recv()
        total = total + frecv[i].astype(jnp.float32)
    for k in range(feat.shape[1] // LANES):
        out[:, k * LANES:(k + 1) * LANES] = total[:, k * LANES:(k + 1) * LANES] * inv

    for copy in gathers:
        copy.wait_send()
    all_of(xwide, NX - 1, xw_sem.at[0])
    for c in range(NCHUNK):
        all_of(xbuf.at[c], NX - 1, x_send.at[c])
        for a in range(2):
            all_of(zbuf.at[a, c], NZ - 1, z_send.at[a, c])
    all_of(rowbuf, NB - 1, row_sem.at[0])
    all_of(massbuf, NB - 1, mass_sem.at[0])
    for i in range(len(steps)):
        mate_copy(i).wait_send()
    for i in range(last):
        out_copy(i).wait_send()


def local(vehicle_emb, request_emb, request_feat, log_supply, log_demand):
    rows, cols, width = BLK * NB, request_emb.shape[0], request_feat.shape[1]
    cw = cols // NCHUNK
    f32, bf16 = jnp.float32, jnp.bfloat16
    dma = pltpu.SemaphoreType.DMA
    scratch = [
        pltpu.VMEM((NB, BLK, vehicle_emb.shape[1]), bf16),
        pltpu.VMEM(request_emb.shape, bf16),
        pltpu.VMEM(request_emb.shape[::-1], bf16),
        pltpu.VMEM(request_feat.shape, bf16),
        pltpu.VMEM((NB, 1, LANES), f32),
        pltpu.VMEM((1, cols), f32),
        pltpu.VMEM((rows, cols), f32),
        pltpu.VMEM((rows, cols), f32),
        pltpu.VMEM((8, cols), f32),
        pltpu.VMEM((8, cols), f32),
        pltpu.VMEM((1, cols), f32),
        pltpu.VMEM((1, cols), f32),
        pltpu.VMEM((NCHUNK, rows, LANES), f32),
        pltpu.VMEM((NCHUNK, rows, LANES), f32),
        pltpu.VMEM((rows, LANES), f32),
        pltpu.VMEM((rows, LANES), f32),
        pltpu.VMEM((NX, 1, cols), f32),
        pltpu.VMEM((NCHUNK, NX, 1, cw), f32),
        pltpu.VMEM((2, NCHUNK, NZ, 1, cw), f32),
        pltpu.VMEM((NB, NB, 1, LANES), f32),
        pltpu.VMEM((NB, 1, LANES), f32),
        pltpu.VMEM((NB, 1, LANES), f32),
        pltpu.VMEM((NB, 1, LANES), f32),
        pltpu.VMEM((NY, 2, BLK, width), f32),
        pltpu.VMEM((NY, BLK, width), f32),
        pltpu.VMEM((NY - 1, BLK, width), bf16),
        pltpu.VMEM((NY - 1, BLK, width), bf16),
        dma((5,)), dma((NB,)), dma((NB,)),
        dma((2,)), dma((NCHUNK,)), dma((NCHUNK,)), dma((2, NCHUNK)), dma((2, NCHUNK)),
        dma((2,)), dma((2,)),
        dma((NY,)), dma((NY,)), dma((NY - 1,)), dma((NY - 1,)),
    ]
    return pl.pallas_call(
        kernel,
        out_shape=jax.ShapeDtypeStruct((BLK, width), f32),
        in_specs=[pl.BlockSpec(memory_space=pl.ANY)] * 5,
        out_specs=pl.BlockSpec(memory_space=pltpu.VMEM),
        scratch_shapes=scratch,
        compiler_params=pltpu.CompilerParams(
            collective_id=0, has_side_effects=True, vmem_limit_bytes=56 * 2**20),
        cost_estimate=pl.CostEstimate(
            flops=2 * rows * cols * (vehicle_emb.shape[1] + width), bytes_accessed=4 * 2**20,
            transcendentals=2 * rows * cols),
        name="sinkhorn_assign",
    )(vehicle_emb, request_emb, request_feat, log_supply.reshape(NB, 1, LANES), log_demand.reshape(1, cols))


def solution(mesh):
    in_specs = (P(("veh", "req"), None), P("req", None), P("req", None), P("veh"), P("req"))
    out_specs = P(("veh", "req"), None)
    return jax.shard_map(local, mesh=mesh, in_specs=in_specs, out_specs=out_specs, check_vma=False)
```

```python
import functools
import math

import jax
import jax.numpy as jnp
from jax import lax
from jax.experimental import pallas as pl
from jax.experimental.pallas import tpu as pltpu
from jax.sharding import PartitionSpec as P

MESH = pl.DeviceIdType.MESH
LOG2E = 1.4426950408889634
NX, NZ, NY = 4, 8, 4
NB = 8
BLK = 128
LANES = 128
NCHUNK = 4
TINY = 1e-30


def score_rows(v_all, r, z, top, acc, slot, scale, first=False, start=0, stop=None):
    width = 512
    v = v_all[slot]
    rows = pl.ds(pl.multiple_of(slot * BLK, BLK), BLK)
    for c in range(start, stop or z.shape[1], width):
        cols = pl.ds(c, width)
        s = lax.dot_general(v, r[cols, :], (((1,), (1,)), ((), ())), preferred_element_type=jnp.float32) * scale
        z[rows, cols] = s
        s = s.reshape(BLK // 8, 8, width)
        peak = jnp.max(s, axis=0)
        if not first:
            old = top[:, cols]
            peak = jnp.maximum(old, peak)
        e = jnp.sum(jnp.exp2(s - peak[None]), axis=0)
        top[:, cols] = peak
        acc[:, cols] = e if first else acc[:, cols] * jnp.exp2(old - peak) + e


def column_lse(top, acc, cols):
    t = top[:, cols]
    peak = jnp.max(t, axis=0, keepdims=True)
    return peak + jnp.log(jnp.sum(acc[:, cols] * jnp.exp2(t - peak), axis=0, keepdims=True)) * LOG2E


def row_pass(z, d, w, m, s, c, cw):
    rows = 64
    kk = cw // LANES

    def step(t, _):
        rr = pl.ds(pl.multiple_of(t * rows, rows), rows)
        ys = [z[rr, pl.ds(c * cw + k * LANES, LANES)] + d[:, pl.ds(c * cw + k * LANES, LANES)] for k in range(kk)]
        peak = functools.reduce(jnp.maximum, ys)
        total = None
        for k in range(kk):
            e = jnp.exp2(ys[k] - peak)
            w[rr, pl.ds(c * cw + k * LANES, LANES)] = e
            total = e if total is None else total + e
        m[c, rr, :] = peak
        s[c, rr, :] = total
        return 0

    lax.fori_loop(0, z.shape[0] // rows, step, 0, unroll=2)


def row_totals(m, s, out):
    for g in range(NB):
        rr = pl.ds(g * BLK, BLK)
        peak = functools.reduce(jnp.maximum, [m[c, rr, :] for c in range(NCHUNK)])
        total = sum(s[c, rr, :] * jnp.exp2(m[c, rr, :] - peak) for c in range(NCHUNK))
        pt, tt = peak.T, total.T
        top = jnp.max(pt, axis=0, keepdims=True)
        out[g] = top + jnp.log(jnp.sum(tt * jnp.exp2(pt - top), axis=0, keepdims=True)) * LOG2E


def spread(sp, col):
    for g in range(NB):
        col[pl.ds(g * BLK, BLK), :] = jnp.broadcast_to(sp[g], (BLK, LANES)).T


def column_sum(w, u, col, c, cw):
    u[c] = jnp.exp2(u[c] + col[...])
    rows = 32
    kk = cw // LANES

    def step(t, accs):
        rr = pl.ds(pl.multiple_of(t * rows, rows), rows)
        ut = u[c, rr, :]
        return tuple(
            a + jnp.sum((w[rr, pl.ds(c * cw + k * LANES, LANES)] * ut).reshape(rows // 8, 8, LANES), axis=0)
            for k, a in enumerate(accs)
        )

    zero = tuple(jnp.zeros((8, LANES), jnp.float32) for _ in range(kk))
    accs = lax.fori_loop(0, w.shape[0] // rows, step, zero, unroll=4)
    return jnp.concatenate([jnp.sum(a, axis=0, keepdims=True) for a in accs], axis=1)


def weight_pass(w, u, gain, t, tm, ms, c, cw):
    rows = 64
    kk = cw // LANES

    def step(i, _):
        rr = pl.ds(pl.multiple_of(i * rows, rows), rows)
        ut = u[c, rr, :]
        peak = total = None
        for k in range(kk):
            cols = pl.ds(c * cw + k * LANES, LANES)
            e = w[rr, cols] * ut * gain[:, cols]
            t[rr, cols] = e
            peak = e if peak is None else jnp.maximum(peak, e)
            total = e if total is None else total + e
        if c > 0:
            peak, total = jnp.maximum(peak, tm[rr, :]), total + ms[rr, :]
        tm[rr, :] = peak
        ms[rr, :] = total
        return 0

    lax.fori_loop(0, w.shape[0] // rows, step, 0)


def block_features(t, tm, feat, row0, rows):
    rr = pl.ds(pl.multiple_of(row0, rows), rows)
    peak = jnp.maximum(jnp.max(tm[rr, :], axis=1, keepdims=True), TINY)
    weights = (t[rr, :] * (1.0 / peak)).astype(jnp.bfloat16)
    return jnp.dot(weights, feat[...], preferred_element_type=jnp.float32) * peak


def lse_parts(parts):
    top = jnp.max(parts, axis=0)
    return top + jnp.log(jnp.sum(jnp.exp2(parts - top[None]), axis=0)) * LOG2E


def kernel(v_hbm, r_hbm, feat_hbm, sup_hbm, dem_hbm, out,
           v_all, r, feat, sup, dem, z, w, top, acc, d, gain, m, s, tm, ms,
           col, xbuf, zbuf, rowbuf, massown, massbuf, sp, fgive, fkeep, fmate, fsend, frecv,
           load_sem, ag_send, ag_recv, relay, x_send, x_recv, z_send, z_recv, row_sem, mass_sem,
           mate_send, mate_recv, f_send, f_recv):
    me, b = lax.axis_index("veh"), lax.axis_index("req")
    zc, xc = me // NX, lax.rem(me, NX)
    y, core = b // 2, lax.rem(b, 2)
    cw = z.shape[1] // NCHUNK
    scale = 3.0 / math.sqrt(v_hbm.shape[1]) * LOG2E

    def x_peer(k):
        return (zc * NX + lax.rem(xc + k, NX), b)

    def z_peer(k):
        return (lax.rem(zc + k, NZ) * NX + xc, b)

    def req_peer(k):
        return (me, lax.rem(b + k, NB))

    def at(dy, dc):
        return lax.rem(y + dy, NY) * 2 + lax.rem(core + dc, 2)

    loads = [
        pltpu.make_async_copy(v_hbm, v_all.at[b], load_sem.at[0]),
        pltpu.make_async_copy(r_hbm, r, load_sem.at[1]),
        pltpu.make_async_copy(sup_hbm, sup, load_sem.at[2]),
        pltpu.make_async_copy(dem_hbm, dem, load_sem.at[3]),
        pltpu.make_async_copy(feat_hbm, feat, load_sem.at[4]),
    ]
    sent = []
    loads[0].start()
    barrier = pltpu.get_barrier_semaphore()
    near_z = (z_peer(1), z_peer(NZ - 1))
    for peer in [req_peer(k) for k in range(1, NB)] + [x_peer(k) for k in range(1, NX)] + list(near_z):
        pl.semaphore_signal(barrier, inc=1, device_id=peer, device_id_type=MESH)
    for load in loads[1:]:
        load.start()
    loads[0].wait()
    pl.semaphore_wait(barrier, NB - 1 + NX - 1 + 2)

    def tell(i):
        for peer in near_z:
            pl.semaphore_signal(relay.at[i], inc=1, device_id=peer, device_id_type=MESH)

    def told(i):
        pl.semaphore_wait(relay.at[i], 2)

    for dy, dc in ((2, 0), (2, 1), (1, 0), (3, 0), (1, 1), (3, 1), (0, 1)):
        copy = pltpu.make_async_remote_copy(
            v_all.at[b], v_all.at[b], ag_send.at[dy, dc], ag_recv.at[(NY - dy) % NY, dc],
            device_id=(me, at(dy, dc)), device_id_type=MESH)
        copy.start()
        sent.append(copy.wait_send)
    tell(0)

    def arrival(dy, dc):
        slot = at(dy, dc)
        pltpu.make_async_copy(v_all.at[slot], v_all.at[slot], ag_recv.at[dy, dc]).wait()
        return slot

    loads[1].wait()
    score_rows(v_all, r, z, top, acc, b, scale, first=True)
    for i, (dy, dc) in enumerate(((0, 1), (1, 0), (3, 0), (1, 1), (3, 1))):
        score_rows(v_all, r, z, top, acc, arrival(dy, dc), scale)
        if i < 3:
            told(i)
        if i < 2:
            tell(i + 1)
    far = (arrival(2, 0), arrival(2, 1))

    def x_start(a, c):
        for k in range(1, NX):
            pltpu.make_async_remote_copy(
                xbuf.at[a, c, NX - 1], xbuf.at[a, c, NX - 1 - k], x_send.at[a, c], x_recv.at[a, c],
                device_id=x_peer(k), device_id_type=MESH).start()
        sent.append(lambda: all_of(xbuf.at[a, c], NX - 1, x_send.at[a, c]))

    def z_start(a, c):
        for k in range(1, NZ):
            pltpu.make_async_remote_copy(
                zbuf.at[a, c, NZ - 1], zbuf.at[a, c, NZ - 1 - k], z_send.at[a, c], z_recv.at[a, c],
                device_id=z_peer(k), device_id_type=MESH).start()
        sent.append(lambda: all_of(zbuf.at[a, c], NZ - 1, z_send.at[a, c]))

    def all_of(buf, n, sem):
        pltpu.make_async_copy(buf.at[pl.ds(0, n)], buf.at[pl.ds(0, n)], sem).wait()

    loads[2].wait()
    loads[3].wait()
    for c in range(NCHUNK):
        for slot in far:
            score_rows(v_all, r, z, top, acc, slot, scale, start=c * cw, stop=(c + 1) * cw)
        xbuf[0, c, NX - 1] = column_lse(top, acc, pl.ds(c * cw, cw))
        x_start(0, c)
    for c in range(NCHUNK):
        all_of(xbuf.at[0, c], NX - 1, x_recv.at[0, c])
        zbuf[0, c, NZ - 1] = lse_parts(xbuf[0, c])
        z_start(0, c)
    for c in range(NCHUNK):
        all_of(zbuf.at[0, c], NZ - 1, z_recv.at[0, c])
        cols = pl.ds(c * cw, cw)
        d[:, cols] = dem[:, cols] * LOG2E - lse_parts(zbuf[0, c])
        row_pass(z, d, w, m, s, c, cw)

    row_totals(m, s, rowbuf.at[NB - 1])
    for k in range(1, NB):
        pltpu.make_async_remote_copy(
            rowbuf.at[NB - 1], rowbuf.at[NB - 1 - k], row_sem.at[0], row_sem.at[1],
            device_id=req_peer(k), device_id_type=MESH).start()
    sent.append(lambda: all_of(rowbuf, NB - 1, row_sem.at[0]))
    all_of(rowbuf, NB - 1, row_sem.at[1])
    sp[...] = sup[...] * LOG2E - lse_parts(rowbuf[...])
    spread(sp, col)

    for c in range(NCHUNK):
        xbuf[1, c, NX - 1] = column_sum(w, m, col, c, cw)
        x_start(1, c)
    for c in range(NCHUNK):
        all_of(xbuf.at[1, c], NX - 1, x_recv.at[1, c])
        zbuf[1, c, NZ - 1] = jnp.sum(xbuf[1, c], axis=0)
        z_start(1, c)
    for c in range(NCHUNK):
        all_of(zbuf.at[1, c], NZ - 1, z_recv.at[1, c])
        cols = pl.ds(c * cw, cw)
        gain[:, cols] = jnp.exp2(dem[:, cols] * LOG2E) / jnp.sum(zbuf[1, c], axis=0)
        weight_pass(w, m, gain, z, tm, ms, c, cw)

    def masses():
        for g in range(NB):
            massown[g] = jnp.sum(ms[pl.ds(g * BLK, BLK), :].T, axis=0, keepdims=True)
        for k in range(1, NB):
            pltpu.make_async_remote_copy(
                massown.at[lax.rem(b + k, NB)], massbuf.at[NB - 1 - k], mass_sem.at[0], mass_sem.at[1],
                device_id=req_peer(k), device_id_type=MESH).start()
        sent.append(lambda: all_of(massbuf, NB - 1, mass_sem.at[0]))
        massbuf[NB - 1] = massown[b]

    def mate_copy(i):
        return pltpu.make_async_remote_copy(
            fgive.at[i], fmate.at[i], mate_send.at[i], mate_recv.at[i],
            device_id=(me, at(0, 1)), device_id_type=MESH)

    def out_copy(i):
        return pltpu.make_async_remote_copy(
            fsend.at[i], frecv.at[i], f_send.at[i], f_recv.at[i],
            device_id=(me, at(steps[i], 0)), device_id_type=MESH)

    def give(i):
        fgive[i] = block_features(z, tm, feat, at(steps[i], 1) * BLK, BLK)
        mate_copy(i).start()
        sent.append(mate_copy(i).wait_send)

    def keep(i):
        fkeep[i] = block_features(z, tm, feat, at(steps[i], 0) * BLK, BLK)

    def pass_on(i):
        mate_copy(i).wait_recv()
        fsend[i] = (fkeep[i] + fmate[i]).astype(jnp.bfloat16)
        out_copy(i).start()
        sent.append(out_copy(i).wait_send)

    steps = (2, 1, 3, 0)
    last = len(steps) - 1
    loads[4].wait()
    give(0)
    give(1)
    give(2)
    keep(0)
    masses()
    keep(1)
    pass_on(0)
    keep(2)
    pass_on(1)
    give(3)
    pass_on(2)
    keep(3)
    all_of(massbuf, NB - 1, mass_sem.at[1])
    mass = jnp.sum(massbuf[...], axis=0)
    inv = 1.0 / jnp.broadcast_to(mass, (BLK, LANES)).T
    mate_copy(last).wait_recv()
    total = fkeep[last] + fmate[last]
    for i in (1, 2, 0):
        out_copy(i).wait_recv()
        total = total + frecv[i].astype(jnp.float32)
    for k in range(feat.shape[1] // LANES):
        out[:, k * LANES:(k + 1) * LANES] = total[:, k * LANES:(k + 1) * LANES] * inv

    for wait in sent:
        wait()


def local(vehicle_emb, request_emb, request_feat, log_supply, log_demand):
    rows, cols, width = BLK * NB, request_emb.shape[0], request_feat.shape[1]
    cw = cols // NCHUNK
    f32, bf16 = jnp.float32, jnp.bfloat16
    dma = pltpu.SemaphoreType.DMA
    scratch = [
        pltpu.VMEM((NB, BLK, vehicle_emb.shape[1]), bf16),
        pltpu.VMEM(request_emb.shape, bf16),
        pltpu.VMEM(request_feat.shape, bf16),
        pltpu.VMEM((NB, 1, LANES), f32),
        pltpu.VMEM((1, cols), f32),
        pltpu.VMEM((rows, cols), f32),
        pltpu.VMEM((rows, cols), f32),
        pltpu.VMEM((8, cols), f32),
        pltpu.VMEM((8, cols), f32),
        pltpu.VMEM((1, cols), f32),
        pltpu.VMEM((1, cols), f32),
        pltpu.VMEM((NCHUNK, rows, LANES), f32),
        pltpu.VMEM((NCHUNK, rows, LANES), f32),
        pltpu.VMEM((rows, LANES), f32),
        pltpu.VMEM((rows, LANES), f32),
        pltpu.VMEM((rows, LANES), f32),
        pltpu.VMEM((2, NCHUNK, NX, 1, cw), f32),
        pltpu.VMEM((2, NCHUNK, NZ, 1, cw), f32),
        pltpu.VMEM((NB, NB, 1, LANES), f32),
        pltpu.VMEM((NB, 1, LANES), f32),
        pltpu.VMEM((NB, 1, LANES), f32),
        pltpu.VMEM((NB, 1, LANES), f32),
        pltpu.VMEM((NY, BLK, width), f32),
        pltpu.VMEM((NY, BLK, width), f32),
        pltpu.VMEM((NY, BLK, width), f32),
        pltpu.VMEM((NY - 1, BLK, width), bf16),
        pltpu.VMEM((NY - 1, BLK, width), bf16),
        dma((5,)), dma((NY, 2)), dma((NY, 2)), pltpu.SemaphoreType.REGULAR((3,)),
        dma((2, NCHUNK)), dma((2, NCHUNK)), dma((2, NCHUNK)), dma((2, NCHUNK)),
        dma((2,)), dma((2,)),
        dma((NY,)), dma((NY,)), dma((NY - 1,)), dma((NY - 1,)),
    ]
    return pl.pallas_call(
        kernel,
        out_shape=jax.ShapeDtypeStruct((BLK, width), f32),
        in_specs=[pl.BlockSpec(memory_space=pl.ANY)] * 5,
        out_specs=pl.BlockSpec(memory_space=pltpu.VMEM),
        scratch_shapes=scratch,
        compiler_params=pltpu.CompilerParams(
            collective_id=0, has_side_effects=True, vmem_limit_bytes=56 * 2**20),
        cost_estimate=pl.CostEstimate(
            flops=2 * rows * cols * (vehicle_emb.shape[1] + width), bytes_accessed=4 * 2**20,
            transcendentals=2 * rows * cols),
        name="sinkhorn_assign",
    )(vehicle_emb, request_emb, request_feat, log_supply.reshape(NB, 1, LANES), log_demand.reshape(1, cols))


def solution(mesh):
    in_specs = (P(("veh", "req"), None), P("req", None), P("req", None), P("veh"), P("req"))
    out_specs = P(("veh", "req"), None)
    return jax.shard_map(local, mesh=mesh, in_specs=in_specs, out_specs=out_specs, check_vma=False)
```

```python
import functools
import math

import jax
import jax.numpy as jnp
from jax import lax
from jax.experimental import pallas as pl
from jax.experimental.pallas import tpu as pltpu
from jax.sharding import PartitionSpec as P

MESH = pl.DeviceIdType.MESH
LOG2E = 1.4426950408889634
NX, NZ, NY = 4, 8, 4
NB = 8
BLK = 128
LANES = 128
NCHUNK = 4
TINY = 1e-30


def score_rows(v_all, r, z, top, acc, slot, n, scale, first=False, start=0, stop=None):
    width = 512
    v = v_all[slot:slot + n].reshape(n * BLK, v_all.shape[2])
    rows = pl.ds(slot * BLK, n * BLK)
    for c in range(start, stop or z.shape[1], width):
        cols = pl.ds(c, width)
        s = lax.dot_general(v, r[cols, :], (((1,), (1,)), ((), ())), preferred_element_type=jnp.float32) * scale
        z[rows, cols] = s
        s = s.reshape(n * BLK // 8, 8, width)
        peak = jnp.max(s, axis=0)
        if not first:
            old = top[:, cols]
            peak = jnp.maximum(old, peak)
        e = jnp.sum(jnp.exp2(s - peak[None]), axis=0)
        top[:, cols] = peak
        acc[:, cols] = e if first else acc[:, cols] * jnp.exp2(old - peak) + e


def column_lse(top, acc, cols):
    t = top[:, cols]
    peak = jnp.max(t, axis=0, keepdims=True)
    return peak + jnp.log(jnp.sum(acc[:, cols] * jnp.exp2(t - peak), axis=0, keepdims=True)) * LOG2E


def row_pass(z, d, w, m, s, c, cw):
    rows = 64
    kk = cw // LANES

    def step(t, _):
        rr = pl.ds(pl.multiple_of(t * rows, rows), rows)
        ys = [z[rr, pl.ds(c * cw + k * LANES, LANES)] + d[:, pl.ds(c * cw + k * LANES, LANES)] for k in range(kk)]
        peak = functools.reduce(jnp.maximum, ys)
        total = None
        for k in range(kk):
            e = jnp.exp2(ys[k] - peak)
            w[rr, pl.ds(c * cw + k * LANES, LANES)] = e
            total = e if total is None else total + e
        m[c, rr, :] = peak
        s[c, rr, :] = total
        return 0

    lax.fori_loop(0, z.shape[0] // rows, step, 0, unroll=2)


def row_totals(m, s, out, place):
    for q in range(NB):
        rr = pl.ds(q * BLK, BLK)
        peak = functools.reduce(jnp.maximum, [m[c, rr, :] for c in range(NCHUNK)])
        total = sum(s[c, rr, :] * jnp.exp2(m[c, rr, :] - peak) for c in range(NCHUNK))
        pt, tt = peak.T, total.T
        top = jnp.max(pt, axis=0, keepdims=True)
        out[place(q)] = top + jnp.log(jnp.sum(tt * jnp.exp2(pt - top), axis=0, keepdims=True)) * LOG2E


def spread(sp, col, place):
    for q in range(NB):
        col[pl.ds(q * BLK, BLK), :] = jnp.broadcast_to(sp[place(q)], (BLK, LANES)).T


def column_sum(w, u, col, c, cw):
    u[c] = jnp.exp2(u[c] + col[...])
    rows = 32
    kk = cw // LANES

    def step(t, accs):
        rr = pl.ds(pl.multiple_of(t * rows, rows), rows)
        ut = u[c, rr, :]
        return tuple(
            a + jnp.sum((w[rr, pl.ds(c * cw + k * LANES, LANES)] * ut).reshape(rows // 8, 8, LANES), axis=0)
            for k, a in enumerate(accs)
        )

    zero = tuple(jnp.zeros((8, LANES), jnp.float32) for _ in range(kk))
    accs = lax.fori_loop(0, w.shape[0] // rows, step, zero, unroll=4)
    return jnp.concatenate([jnp.sum(a, axis=0, keepdims=True) for a in accs], axis=1)


def weight_pass(w, u, gain, tm, ms, c, cw):
    rows = 64
    kk = cw // LANES

    def step(i, _):
        rr = pl.ds(pl.multiple_of(i * rows, rows), rows)
        peak = total = None
        for k in range(kk):
            cols = pl.ds(c * cw + k * LANES, LANES)
            e = w[rr, cols] * gain[:, cols]
            peak = e if peak is None else jnp.maximum(peak, e)
            total = e if total is None else total + e
        ut = u[c, rr, :]
        peak, total = peak * ut, total * ut
        if c > 0:
            peak, total = jnp.maximum(peak, tm[rr, :]), total + ms[rr, :]
        tm[rr, :] = peak
        ms[rr, :] = total
        return 0

    lax.fori_loop(0, w.shape[0] // rows, step, 0)


def block_features(w, u, gain, tm, feat, packed, row0, rows, cw):
    rr = pl.ds(row0, rows)
    peak = jnp.maximum(jnp.max(tm[rr, :], axis=1, keepdims=True), TINY)
    inv = 1.0 / peak
    for c in range(NCHUNK):
        a = u[c, rr, :] * inv
        for k in range(cw // LANES):
            cols = pl.ds(c * cw + k * LANES, LANES)
            packed[:, cols] = (w[rr, cols] * a * gain[:, cols]).astype(jnp.bfloat16)
    return jnp.dot(packed[...], feat[...], preferred_element_type=jnp.float32) * peak


def lse_parts(parts):
    top = jnp.max(parts, axis=0)
    return top + jnp.log(jnp.sum(jnp.exp2(parts - top[None]), axis=0)) * LOG2E


def kernel(v_hbm, r_hbm, feat_hbm, sup_hbm, dem_hbm, out,
           v_all, r, feat, sup, dem, z, w, top, acc, d, gain, m, s, tm, ms,
           col, xbuf, zbuf, rowbuf, massown, massbuf, sp, packed, fgive, fkeep, fmate, fsend, frecv,
           load_sem, ag_send, ag_recv, relay, x_send, x_recv, z_send, z_recv, row_sem, mass_sem,
           mate_send, mate_recv, f_send, f_recv):
    me, b = lax.axis_index("veh"), lax.axis_index("req")
    zc, xc = me // NX, lax.rem(me, NX)
    y, core = b // 2, lax.rem(b, 2)
    cw = z.shape[1] // NCHUNK
    scale = 3.0 / math.sqrt(v_hbm.shape[1]) * LOG2E

    def x_peer(k):
        return (zc * NX + lax.rem(xc + k, NX), b)

    def z_peer(k):
        return (lax.rem(zc + k, NZ) * NX + xc, b)

    def req_peer(k):
        return (me, lax.rem(b + k, NB))

    def at(dy, dc):
        return lax.rem(y + dy, NY) * 2 + lax.rem(core + dc, 2)

    def place(q):
        return at(q // 2, q % 2)

    loads = [
        pltpu.make_async_copy(v_hbm, v_all.at[0], load_sem.at[0]),
        pltpu.make_async_copy(r_hbm, r, load_sem.at[1]),
        pltpu.make_async_copy(sup_hbm, sup, load_sem.at[2]),
        pltpu.make_async_copy(dem_hbm, dem, load_sem.at[3]),
        pltpu.make_async_copy(feat_hbm, feat, load_sem.at[4]),
    ]
    sent = []
    loads[0].start()
    barrier = pltpu.get_barrier_semaphore()
    near_z = (z_peer(1), z_peer(NZ - 1))
    for peer in [req_peer(k) for k in range(1, NB)] + [x_peer(k) for k in range(1, NX)] + list(near_z):
        pl.semaphore_signal(barrier, inc=1, device_id=peer, device_id_type=MESH)
    for load in loads[1:]:
        load.start()
    loads[0].wait()
    pl.semaphore_wait(barrier, NB - 1 + NX - 1 + 2)

    def tell(i):
        for peer in near_z:
            pl.semaphore_signal(relay.at[i], inc=1, device_id=peer, device_id_type=MESH)

    def told(i):
        pl.semaphore_wait(relay.at[i], 2)

    for q in (4, 5, 2, 6, 3, 7, 1):
        dy, dc = q // 2, q % 2
        there = (NY - dy) % NY * 2 + dc
        copy = pltpu.make_async_remote_copy(
            v_all.at[0], v_all.at[there], ag_send.at[q], ag_recv.at[there],
            device_id=(me, at(dy, dc)), device_id_type=MESH)
        copy.start()
        sent.append(copy.wait_send)
    tell(0)

    def arrived(*blocks):
        for q in blocks:
            pltpu.make_async_copy(v_all.at[q], v_all.at[q], ag_recv.at[q]).wait()

    loads[1].wait()
    score_rows(v_all, r, z, top, acc, 0, 1, scale, first=True)
    told(0)
    tell(1)
    arrived(1)
    score_rows(v_all, r, z, top, acc, 1, 1, scale)
    told(1)
    tell(2)
    arrived(2, 3)
    score_rows(v_all, r, z, top, acc, 2, 2, scale)
    told(2)
    arrived(6, 7)
    score_rows(v_all, r, z, top, acc, 6, 2, scale)
    arrived(4, 5)

    def x_start(a, c):
        for k in range(1, NX):
            pltpu.make_async_remote_copy(
                xbuf.at[a, c, NX - 1], xbuf.at[a, c, NX - 1 - k], x_send.at[a, c], x_recv.at[a, c],
                device_id=x_peer(k), device_id_type=MESH).start()
        sent.append(lambda: all_of(xbuf.at[a, c], NX - 1, x_send.at[a, c]))

    def z_start(a, c):
        for k in range(1, NZ):
            pltpu.make_async_remote_copy(
                zbuf.at[a, c, NZ - 1], zbuf.at[a, c, NZ - 1 - k], z_send.at[a, c], z_recv.at[a, c],
                device_id=z_peer(k), device_id_type=MESH).start()
        sent.append(lambda: all_of(zbuf.at[a, c], NZ - 1, z_send.at[a, c]))

    def all_of(buf, n, sem):
        pltpu.make_async_copy(buf.at[pl.ds(0, n)], buf.at[pl.ds(0, n)], sem).wait()

    loads[2].wait()
    loads[3].wait()
    for c in range(NCHUNK):
        score_rows(v_all, r, z, top, acc, 4, 2, scale, start=c * cw, stop=(c + 1) * cw)
        xbuf[0, c, NX - 1] = column_lse(top, acc, pl.ds(c * cw, cw))
        x_start(0, c)
    for c in range(NCHUNK):
        all_of(xbuf.at[0, c], NX - 1, x_recv.at[0, c])
        zbuf[0, c, NZ - 1] = lse_parts(xbuf[0, c])
        z_start(0, c)
    for c in range(NCHUNK):
        all_of(zbuf.at[0, c], NZ - 1, z_recv.at[0, c])
        cols = pl.ds(c * cw, cw)
        d[:, cols] = dem[:, cols] * LOG2E - lse_parts(zbuf[0, c])
        row_pass(z, d, w, m, s, c, cw)

    row_totals(m, s, rowbuf.at[NB - 1], place)
    for k in range(1, NB):
        pltpu.make_async_remote_copy(
            rowbuf.at[NB - 1], rowbuf.at[NB - 1 - k], row_sem.at[0], row_sem.at[1],
            device_id=req_peer(k), device_id_type=MESH).start()
    sent.append(lambda: all_of(rowbuf, NB - 1, row_sem.at[0]))
    all_of(rowbuf, NB - 1, row_sem.at[1])
    sp[...] = sup[...] * LOG2E - lse_parts(rowbuf[...])
    spread(sp, col, place)

    for c in range(NCHUNK):
        xbuf[1, c, NX - 1] = column_sum(w, m, col, c, cw)
        x_start(1, c)
    for c in range(NCHUNK):
        all_of(xbuf.at[1, c], NX - 1, x_recv.at[1, c])
        zbuf[1, c, NZ - 1] = jnp.sum(xbuf[1, c], axis=0)
        z_start(1, c)
    for c in range(NCHUNK):
        all_of(zbuf.at[1, c], NZ - 1, z_recv.at[1, c])
        cols = pl.ds(c * cw, cw)
        gain[:, cols] = jnp.exp2(dem[:, cols] * LOG2E) / jnp.sum(zbuf[1, c], axis=0)
        weight_pass(w, m, gain, tm, ms, c, cw)

    for q in range(NB):
        massown[q] = jnp.sum(ms[pl.ds(q * BLK, BLK), :].T, axis=0, keepdims=True)
    for q in range(1, NB):
        there = (NY - q // 2) % NY * 2 + q % 2
        pltpu.make_async_remote_copy(
            massown.at[q], massbuf.at[there], mass_sem.at[0], mass_sem.at[1],
            device_id=(me, place(q)), device_id_type=MESH).start()
    others = massbuf.at[pl.ds(1, NB - 1)]
    sent.append(lambda: pltpu.make_async_copy(others, others, mass_sem.at[0]).wait())
    massbuf[0] = massown[0]

    def mate_copy(dy):
        return pltpu.make_async_remote_copy(
            fgive.at[dy], fmate.at[dy], mate_send.at[dy], mate_recv.at[dy],
            device_id=(me, at(0, 1)), device_id_type=MESH)

    def out_copy(dy):
        return pltpu.make_async_remote_copy(
            fsend.at[dy - 1], frecv.at[dy - 1], f_send.at[dy - 1], f_recv.at[dy - 1],
            device_id=(me, at(dy, 0)), device_id_type=MESH)

    def unit(dy, i):
        f = block_features(w, m, gain, tm, feat, packed.at[i % 2], dy * 2 * BLK, 2 * BLK, cw)
        fgive[dy] = f[BLK:]
        mate_copy(dy).start()
        fkeep[dy] = f[:BLK]

    def pass_on(dy):
        mate_copy(dy).wait_recv()
        fsend[dy - 1] = (fkeep[dy] + fmate[dy]).astype(jnp.bfloat16)
        out_copy(dy).start()

    loads[4].wait()
    unit(2, 0)
    unit(1, 1)
    pass_on(2)
    unit(3, 2)
    pass_on(1)
    unit(0, 3)
    pass_on(3)
    for wait in sent:
        wait()
    pltpu.make_async_copy(others, others, mass_sem.at[1]).wait()
    mass = jnp.sum(massbuf[...], axis=0)
    inv = 1.0 / jnp.broadcast_to(mass, (BLK, LANES)).T
    mate_copy(0).wait_recv()
    total = fkeep[0] + fmate[0]
    for dy in (1, 2, 3):
        out_copy(dy).wait_recv()
        total = total + frecv[dy - 1].astype(jnp.float32)
    for k in range(feat.shape[1] // LANES):
        out[:, k * LANES:(k + 1) * LANES] = total[:, k * LANES:(k + 1) * LANES] * inv
    for dy in range(NY):
        mate_copy(dy).wait_send()
        if dy:
            out_copy(dy).wait_send()


def local(vehicle_emb, request_emb, request_feat, log_supply, log_demand):
    rows, cols, width = BLK * NB, request_emb.shape[0], request_feat.shape[1]
    cw = cols // NCHUNK
    f32, bf16 = jnp.float32, jnp.bfloat16
    dma = pltpu.SemaphoreType.DMA
    scratch = [
        pltpu.VMEM((NB, BLK, vehicle_emb.shape[1]), bf16),
        pltpu.VMEM(request_emb.shape, bf16),
        pltpu.VMEM(request_feat.shape, bf16),
        pltpu.VMEM((NB, 1, LANES), f32),
        pltpu.VMEM((1, cols), f32),
        pltpu.VMEM((rows, cols), f32),
        pltpu.VMEM((rows, cols), f32),
        pltpu.VMEM((8, cols), f32),
        pltpu.VMEM((8, cols), f32),
        pltpu.VMEM((1, cols), f32),
        pltpu.VMEM((1, cols), f32),
        pltpu.VMEM((NCHUNK, rows, LANES), f32),
        pltpu.VMEM((NCHUNK, rows, LANES), f32),
        pltpu.VMEM((rows, LANES), f32),
        pltpu.VMEM((rows, LANES), f32),
        pltpu.VMEM((rows, LANES), f32),
        pltpu.VMEM((2, NCHUNK, NX, 1, cw), f32),
        pltpu.VMEM((2, NCHUNK, NZ, 1, cw), f32),
        pltpu.VMEM((NB, NB, 1, LANES), f32),
        pltpu.VMEM((NB, 1, LANES), f32),
        pltpu.VMEM((NB, 1, LANES), f32),
        pltpu.VMEM((NB, 1, LANES), f32),
        pltpu.VMEM((2, 2 * BLK, cols), bf16),
        pltpu.VMEM((NY, BLK, width), f32),
        pltpu.VMEM((NY, BLK, width), f32),
        pltpu.VMEM((NY, BLK, width), f32),
        pltpu.VMEM((NY - 1, BLK, width), bf16),
        pltpu.VMEM((NY - 1, BLK, width), bf16),
        dma((5,)), dma((NB,)), dma((NB,)), pltpu.SemaphoreType.REGULAR((3,)),
        dma((2, NCHUNK)), dma((2, NCHUNK)), dma((2, NCHUNK)), dma((2, NCHUNK)),
        dma((2,)), dma((2,)),
        dma((NY,)), dma((NY,)), dma((NY - 1,)), dma((NY - 1,)),
    ]
    return pl.pallas_call(
        kernel,
        out_shape=jax.ShapeDtypeStruct((BLK, width), f32),
        in_specs=[pl.BlockSpec(memory_space=pl.ANY)] * 5,
        out_specs=pl.BlockSpec(memory_space=pltpu.VMEM),
        scratch_shapes=scratch,
        compiler_params=pltpu.CompilerParams(
            collective_id=0, has_side_effects=True, vmem_limit_bytes=56 * 2**20),
        cost_estimate=pl.CostEstimate(
            flops=2 * rows * cols * (vehicle_emb.shape[1] + width), bytes_accessed=4 * 2**20,
            transcendentals=2 * rows * cols),
        name="sinkhorn_assign",
    )(vehicle_emb, request_emb, request_feat, log_supply.reshape(NB, 1, LANES), log_demand.reshape(1, cols))


def solution(mesh):
    in_specs = (P(("veh", "req"), None), P("req", None), P("req", None), P("veh"), P("req"))
    out_specs = P(("veh", "req"), None)
    return jax.shard_map(local, mesh=mesh, in_specs=in_specs, out_specs=out_specs, check_vma=False)
```

```python
import functools
import math

import jax
import jax.numpy as jnp
from jax import lax
from jax.experimental import pallas as pl
from jax.experimental.pallas import tpu as pltpu
from jax.sharding import PartitionSpec as P

MESH = pl.DeviceIdType.MESH
LOG2E = 1.4426950408889634
NX, NZ, NY = 4, 8, 4
NB = 8
BLK = 128
LANES = 128
NCHUNK = 4
TINY = 1e-30


def score_rows(v_all, r, z, top, acc, slot, n, scale, first=False, start=0, stop=None):
    width = 512
    v = v_all[slot:slot + n].reshape(n * BLK, v_all.shape[2])
    rows = pl.ds(slot * BLK, n * BLK)
    for c in range(start, stop or z.shape[1], width):
        cols = pl.ds(c, width)
        s = lax.dot_general(v, r[cols, :], (((1,), (1,)), ((), ())), preferred_element_type=jnp.float32) * scale
        z[rows, cols] = s
        s = s.reshape(n * BLK // 8, 8, width)
        peak = jnp.max(s, axis=0)
        if not first:
            old = top[:, cols]
            peak = jnp.maximum(old, peak)
        e = jnp.sum(jnp.exp2(s - peak[None]), axis=0)
        top[:, cols] = peak
        acc[:, cols] = e if first else acc[:, cols] * jnp.exp2(old - peak) + e


def column_lse(top, acc, cols):
    t = top[:, cols]
    peak = jnp.max(t, axis=0, keepdims=True)
    return peak + jnp.log(jnp.sum(acc[:, cols] * jnp.exp2(t - peak), axis=0, keepdims=True)) * LOG2E


def row_pass(z, d, w, m, s, c, cw):
    rows = 64
    kk = cw // LANES

    def step(t, _):
        rr = pl.ds(pl.multiple_of(t * rows, rows), rows)
        ys = [z[rr, pl.ds(c * cw + k * LANES, LANES)] + d[:, pl.ds(c * cw + k * LANES, LANES)] for k in range(kk)]
        peak = functools.reduce(jnp.maximum, ys)
        total = None
        for k in range(kk):
            e = jnp.exp2(ys[k] - peak)
            w[rr, pl.ds(c * cw + k * LANES, LANES)] = e
            total = e if total is None else total + e
        m[c, rr, :] = peak
        s[c, rr, :] = total
        return 0

    lax.fori_loop(0, z.shape[0] // rows, step, 0, unroll=2)


def row_totals(m, s, out, place):
    for q in range(NB):
        rr = pl.ds(q * BLK, BLK)
        peak = functools.reduce(jnp.maximum, [m[c, rr, :] for c in range(NCHUNK)])
        total = sum(s[c, rr, :] * jnp.exp2(m[c, rr, :] - peak) for c in range(NCHUNK))
        pt, tt = peak.T, total.T
        top = jnp.max(pt, axis=0, keepdims=True)
        out[place(q)] = top + jnp.log(jnp.sum(tt * jnp.exp2(pt - top), axis=0, keepdims=True)) * LOG2E


def spread(sp, col, place):
    for q in range(NB):
        col[pl.ds(q * BLK, BLK), :] = jnp.broadcast_to(sp[place(q)], (BLK, LANES)).T


def column_sum(w, u, col, c, cw):
    u[c] = jnp.exp2(u[c] + col[...])
    rows = 32
    kk = cw // LANES

    def step(t, accs):
        rr = pl.ds(pl.multiple_of(t * rows, rows), rows)
        ut = u[c, rr, :]
        return tuple(
            a + jnp.sum((w[rr, pl.ds(c * cw + k * LANES, LANES)] * ut).reshape(rows // 8, 8, LANES), axis=0)
            for k, a in enumerate(accs)
        )

    zero = tuple(jnp.zeros((8, LANES), jnp.float32) for _ in range(kk))
    accs = lax.fori_loop(0, w.shape[0] // rows, step, zero, unroll=4)
    return jnp.concatenate([jnp.sum(a, axis=0, keepdims=True) for a in accs], axis=1)


def weight_pass(w, gain, tm, ms, c, cw):
    rows = 32
    kk = cw // LANES

    def step(i, _):
        rr = pl.ds(pl.multiple_of(i * rows, rows), rows)
        peak = total = None
        for k in range(kk):
            cols = pl.ds(c * cw + k * LANES, LANES)
            e = w[rr, cols] * gain[:, cols]
            peak = e if peak is None else jnp.maximum(peak, e)
            total = e if total is None else total + e
        tm[c, rr, :] = peak
        ms[c, rr, :] = total
        return 0

    lax.fori_loop(0, w.shape[0] // rows, step, 0, unroll=4)


def block_mass(u, ms, row0):
    rr = pl.ds(row0, BLK)
    return jnp.sum(sum(ms[c, rr, :] * u[c, rr, :] for c in range(NCHUNK)).T, axis=0, keepdims=True)


def block_features(w, u, gain, tm, feat, row0, rows, cw):
    rr = pl.ds(row0, rows)
    peak = functools.reduce(jnp.maximum, [tm[c, rr, :] * u[c, rr, :] for c in range(NCHUNK)])
    peak = jnp.maximum(jnp.max(peak, axis=1, keepdims=True), TINY)
    inv = 1.0 / peak
    weights = []
    for c in range(NCHUNK):
        a = u[c, rr, :] * inv
        for k in range(cw // LANES):
            cols = pl.ds(c * cw + k * LANES, LANES)
            weights.append((w[rr, cols] * a * gain[:, cols]).astype(jnp.bfloat16))
    return jnp.dot(jnp.concatenate(weights, axis=1), feat[...], preferred_element_type=jnp.float32) * peak


def lse_parts(parts):
    top = jnp.max(parts, axis=0)
    return top + jnp.log(jnp.sum(jnp.exp2(parts - top[None]), axis=0)) * LOG2E


def kernel(v_hbm, r_hbm, feat_hbm, sup_hbm, dem_hbm, out,
           v_all, r, feat, sup, dem, z, w, top, acc, d, gain, m, s, tm,
           col, xbuf, zbuf, rowbuf, massown, massbuf, sp, fgive, fkeep, fmate, fsend, frecv,
           load_sem, ag_send, ag_recv, relay, x_send, x_recv, z_send, z_recv, row_sem, mass_sem,
           mate_send, mate_recv, f_send, f_recv):
    me, b = lax.axis_index("veh"), lax.axis_index("req")
    zc, xc = me // NX, lax.rem(me, NX)
    y, core = b // 2, lax.rem(b, 2)
    cw = z.shape[1] // NCHUNK
    scale = 3.0 / math.sqrt(v_hbm.shape[1]) * LOG2E

    def x_peer(k):
        return (zc * NX + lax.rem(xc + k, NX), b)

    def z_peer(k):
        return (lax.rem(zc + k, NZ) * NX + xc, b)

    def req_peer(k):
        return (me, lax.rem(b + k, NB))

    def at(dy, dc):
        return lax.rem(y + dy, NY) * 2 + lax.rem(core + dc, 2)

    def place(q):
        return at(q // 2, q % 2)

    loads = [
        pltpu.make_async_copy(v_hbm, v_all.at[0], load_sem.at[0]),
        pltpu.make_async_copy(r_hbm, r, load_sem.at[1]),
        pltpu.make_async_copy(sup_hbm, sup, load_sem.at[2]),
        pltpu.make_async_copy(dem_hbm, dem, load_sem.at[3]),
        pltpu.make_async_copy(feat_hbm, feat, load_sem.at[4]),
    ]
    sent = []
    loads[0].start()
    barrier = pltpu.get_barrier_semaphore()
    near_z = (z_peer(1), z_peer(NZ - 1))
    for peer in [req_peer(k) for k in range(1, NB)] + [x_peer(k) for k in range(1, NX)] + list(near_z):
        pl.semaphore_signal(barrier, inc=1, device_id=peer, device_id_type=MESH)
    for load in loads[1:]:
        load.start()
    loads[0].wait()
    pl.semaphore_wait(barrier, NB - 1 + NX - 1 + 2)

    def tell(i):
        for peer in near_z:
            pl.semaphore_signal(relay.at[i], inc=1, device_id=peer, device_id_type=MESH)

    def told(i):
        pl.semaphore_wait(relay.at[i], 2)

    for q in (4, 5, 2, 6, 3, 7, 1):
        dy, dc = q // 2, q % 2
        there = (NY - dy) % NY * 2 + dc
        copy = pltpu.make_async_remote_copy(
            v_all.at[0], v_all.at[there], ag_send.at[q], ag_recv.at[there],
            device_id=(me, at(dy, dc)), device_id_type=MESH)
        copy.start()
        sent.append(copy.wait_send)
    tell(0)

    def arrived(*blocks):
        for q in blocks:
            pltpu.make_async_copy(v_all.at[q], v_all.at[q], ag_recv.at[q]).wait()

    loads[1].wait()
    score_rows(v_all, r, z, top, acc, 0, 1, scale, first=True)
    told(0)
    tell(1)
    arrived(1)
    score_rows(v_all, r, z, top, acc, 1, 1, scale)
    told(1)
    tell(2)
    arrived(2, 3)
    score_rows(v_all, r, z, top, acc, 2, 2, scale)
    told(2)
    arrived(6, 7)
    score_rows(v_all, r, z, top, acc, 6, 2, scale)
    arrived(4, 5)

    def x_start(a, c):
        for k in range(1, NX):
            pltpu.make_async_remote_copy(
                xbuf.at[a, c, NX - 1], xbuf.at[a, c, NX - 1 - k], x_send.at[a, c], x_recv.at[a, c],
                device_id=x_peer(k), device_id_type=MESH).start()
        sent.append(lambda: all_of(xbuf.at[a, c], NX - 1, x_send.at[a, c]))

    def z_start(a, c):
        for k in range(1, NZ):
            pltpu.make_async_remote_copy(
                zbuf.at[a, c, NZ - 1], zbuf.at[a, c, NZ - 1 - k], z_send.at[a, c], z_recv.at[a, c],
                device_id=z_peer(k), device_id_type=MESH).start()
        sent.append(lambda: all_of(zbuf.at[a, c], NZ - 1, z_send.at[a, c]))

    def all_of(buf, n, sem):
        pltpu.make_async_copy(buf.at[pl.ds(0, n)], buf.at[pl.ds(0, n)], sem).wait()

    loads[2].wait()
    loads[3].wait()
    for c in range(NCHUNK):
        score_rows(v_all, r, z, top, acc, 4, 2, scale, start=c * cw, stop=(c + 1) * cw)
        xbuf[0, c, NX - 1] = column_lse(top, acc, pl.ds(c * cw, cw))
        x_start(0, c)
    for c in range(NCHUNK):
        all_of(xbuf.at[0, c], NX - 1, x_recv.at[0, c])
        zbuf[0, c, NZ - 1] = lse_parts(xbuf[0, c])
        z_start(0, c)
    for c in range(NCHUNK):
        all_of(zbuf.at[0, c], NZ - 1, z_recv.at[0, c])
        cols = pl.ds(c * cw, cw)
        d[:, cols] = dem[:, cols] * LOG2E - lse_parts(zbuf[0, c])
        row_pass(z, d, w, m, s, c, cw)

    row_totals(m, s, rowbuf.at[NB - 1], place)
    for k in range(1, NB):
        pltpu.make_async_remote_copy(
            rowbuf.at[NB - 1], rowbuf.at[NB - 1 - k], row_sem.at[0], row_sem.at[1],
            device_id=req_peer(k), device_id_type=MESH).start()
    sent.append(lambda: all_of(rowbuf, NB - 1, row_sem.at[0]))
    all_of(rowbuf, NB - 1, row_sem.at[1])
    sp[...] = sup[...] * LOG2E - lse_parts(rowbuf[...])
    spread(sp, col, place)

    for c in range(NCHUNK):
        xbuf[1, c, NX - 1] = column_sum(w, m, col, c, cw)
        x_start(1, c)
    for c in range(NCHUNK):
        all_of(xbuf.at[1, c], NX - 1, x_recv.at[1, c])
        zbuf[1, c, NZ - 1] = jnp.sum(xbuf[1, c], axis=0)
        z_start(1, c)
    for c in range(NCHUNK):
        all_of(zbuf.at[1, c], NZ - 1, z_recv.at[1, c])
        cols = pl.ds(c * cw, cw)
        gain[:, cols] = jnp.exp2(dem[:, cols] * LOG2E) / jnp.sum(zbuf[1, c], axis=0)
        weight_pass(w, gain, tm, s, c, cw)

    for q in range(NB):
        massown[q] = block_mass(m, s, q * BLK)
    for q in range(1, NB):
        there = (NY - q // 2) % NY * 2 + q % 2
        pltpu.make_async_remote_copy(
            massown.at[q], massbuf.at[there], mass_sem.at[0], mass_sem.at[1],
            device_id=(me, place(q)), device_id_type=MESH).start()
    others = massbuf.at[pl.ds(1, NB - 1)]
    sent.append(lambda: pltpu.make_async_copy(others, others, mass_sem.at[0]).wait())
    massbuf[0] = massown[0]

    def mate_copy(dy):
        return pltpu.make_async_remote_copy(
            fgive.at[dy], fmate.at[dy], mate_send.at[dy], mate_recv.at[dy],
            device_id=(me, at(0, 1)), device_id_type=MESH)

    def out_copy(dy):
        return pltpu.make_async_remote_copy(
            fsend.at[dy - 1], frecv.at[dy - 1], f_send.at[dy - 1], f_recv.at[dy - 1],
            device_id=(me, at(dy, 0)), device_id_type=MESH)

    def unit(dy):
        f = block_features(w, m, gain, tm, feat, dy * 2 * BLK, 2 * BLK, cw)
        fgive[dy] = f[BLK:]
        mate_copy(dy).start()
        fkeep[dy] = f[:BLK]

    def pass_on(dy):
        mate_copy(dy).wait_recv()
        fsend[dy - 1] = (fkeep[dy] + fmate[dy]).astype(jnp.bfloat16)
        out_copy(dy).start()

    loads[4].wait()
    unit(2)
    unit(1)
    pass_on(2)
    unit(3)
    pass_on(1)
    unit(0)
    pass_on(3)
    for wait in sent:
        wait()
    pltpu.make_async_copy(others, others, mass_sem.at[1]).wait()
    mass = jnp.sum(massbuf[...], axis=0)
    inv = 1.0 / jnp.broadcast_to(mass, (BLK, LANES)).T
    mate_copy(0).wait_recv()
    total = fkeep[0] + fmate[0]
    for dy in (1, 2, 3):
        out_copy(dy).wait_recv()
        total = total + frecv[dy - 1].astype(jnp.float32)
    for k in range(feat.shape[1] // LANES):
        out[:, k * LANES:(k + 1) * LANES] = total[:, k * LANES:(k + 1) * LANES] * inv
    for dy in range(NY):
        mate_copy(dy).wait_send()
        if dy:
            out_copy(dy).wait_send()


def local(vehicle_emb, request_emb, request_feat, log_supply, log_demand):
    rows, cols, width = BLK * NB, request_emb.shape[0], request_feat.shape[1]
    cw = cols // NCHUNK
    f32, bf16 = jnp.float32, jnp.bfloat16
    dma = pltpu.SemaphoreType.DMA
    scratch = [
        pltpu.VMEM((NB, BLK, vehicle_emb.shape[1]), bf16),
        pltpu.VMEM(request_emb.shape, bf16),
        pltpu.VMEM(request_feat.shape, bf16),
        pltpu.VMEM((NB, 1, LANES), f32),
        pltpu.VMEM((1, cols), f32),
        pltpu.VMEM((rows, cols), f32),
        pltpu.VMEM((rows, cols), f32),
        pltpu.VMEM((8, cols), f32),
        pltpu.VMEM((8, cols), f32),
        pltpu.VMEM((1, cols), f32),
        pltpu.VMEM((1, cols), f32),
        pltpu.VMEM((NCHUNK, rows, LANES), f32),
        pltpu.VMEM((NCHUNK, rows, LANES), f32),
        pltpu.VMEM((NCHUNK, rows, LANES), f32),
        pltpu.VMEM((rows, LANES), f32),
        pltpu.VMEM((2, NCHUNK, NX, 1, cw), f32),
        pltpu.VMEM((2, NCHUNK, NZ, 1, cw), f32),
        pltpu.VMEM((NB, NB, 1, LANES), f32),
        pltpu.VMEM((NB, 1, LANES), f32),
        pltpu.VMEM((NB, 1, LANES), f32),
        pltpu.VMEM((NB, 1, LANES), f32),
        pltpu.VMEM((NY, BLK, width), f32),
        pltpu.VMEM((NY, BLK, width), f32),
        pltpu.VMEM((NY, BLK, width), f32),
        pltpu.VMEM((NY - 1, BLK, width), bf16),
        pltpu.VMEM((NY - 1, BLK, width), bf16),
        dma((5,)), dma((NB,)), dma((NB,)), pltpu.SemaphoreType.REGULAR((3,)),
        dma((2, NCHUNK)), dma((2, NCHUNK)), dma((2, NCHUNK)), dma((2, NCHUNK)),
        dma((2,)), dma((2,)),
        dma((NY,)), dma((NY,)), dma((NY - 1,)), dma((NY - 1,)),
    ]
    return pl.pallas_call(
        kernel,
        out_shape=jax.ShapeDtypeStruct((BLK, width), f32),
        in_specs=[pl.BlockSpec(memory_space=pl.ANY)] * 5,
        out_specs=pl.BlockSpec(memory_space=pltpu.VMEM),
        scratch_shapes=scratch,
        compiler_params=pltpu.CompilerParams(
            collective_id=0, has_side_effects=True, vmem_limit_bytes=56 * 2**20),
        cost_estimate=pl.CostEstimate(
            flops=2 * rows * cols * (vehicle_emb.shape[1] + width), bytes_accessed=4 * 2**20,
            transcendentals=2 * rows * cols),
        name="sinkhorn_assign",
    )(vehicle_emb, request_emb, request_feat, log_supply.reshape(NB, 1, LANES), log_demand.reshape(1, cols))


def solution(mesh):
    in_specs = (P(("veh", "req"), None), P("req", None), P("req", None), P("veh"), P("req"))
    out_specs = P(("veh", "req"), None)
    return jax.shard_map(local, mesh=mesh, in_specs=in_specs, out_specs=out_specs, check_vma=False)
```

```python
import functools
import math

import jax
import jax.numpy as jnp
from jax import lax
from jax.experimental import pallas as pl
from jax.experimental.pallas import tpu as pltpu
from jax.sharding import PartitionSpec as P

MESH = pl.DeviceIdType.MESH
LOG2E = 1.4426950408889634
NX, NZ, NY = 4, 8, 4
NB = 8
BLK = 128
LANES = 128
NCHUNK = 4
TINY = 1e-30


def score_rows(v_all, r, z, top, acc, slot, n, scale, first=False, start=0, stop=None):
    width = 512
    v = v_all[slot:slot + n].reshape(n * BLK, v_all.shape[2])
    rows = pl.ds(slot * BLK, n * BLK)
    for c in range(start, stop or z.shape[1], width):
        cols = pl.ds(c, width)
        s = lax.dot_general(v, r[cols, :], (((1,), (1,)), ((), ())), preferred_element_type=jnp.float32) * scale
        z[rows, cols] = s
        s = s.reshape(n * BLK // 8, 8, width)
        peak = jnp.max(s, axis=0)
        if not first:
            old = top[:, cols]
            peak = jnp.maximum(old, peak)
        e = jnp.sum(jnp.exp2(s - peak[None]), axis=0)
        top[:, cols] = peak
        acc[:, cols] = e if first else acc[:, cols] * jnp.exp2(old - peak) + e


def column_lse(top, acc, cols):
    t = top[:, cols]
    peak = jnp.max(t, axis=0, keepdims=True)
    return peak + jnp.log(jnp.sum(acc[:, cols] * jnp.exp2(t - peak), axis=0, keepdims=True)) * LOG2E


def row_pass(z, d, w, m, s, c, cw):
    rows = 64
    kk = cw // LANES

    def step(t, _):
        rr = pl.ds(pl.multiple_of(t * rows, rows), rows)
        ys = [z[rr, pl.ds(c * cw + k * LANES, LANES)] + d[:, pl.ds(c * cw + k * LANES, LANES)] for k in range(kk)]
        peak = functools.reduce(jnp.maximum, ys)
        total = None
        for k in range(kk):
            e = jnp.exp2(ys[k] - peak)
            w[rr, pl.ds(c * cw + k * LANES, LANES)] = e
            total = e if total is None else total + e
        m[c, rr, :] = peak
        s[c, rr, :] = total
        return 0

    lax.fori_loop(0, z.shape[0] // rows, step, 0, unroll=2)


def row_totals(m, s, out, place):
    for q in range(NB):
        rr = pl.ds(q * BLK, BLK)
        peak = functools.reduce(jnp.maximum, [m[c, rr, :] for c in range(NCHUNK)])
        total = sum(s[c, rr, :] * jnp.exp2(m[c, rr, :] - peak) for c in range(NCHUNK))
        pt, tt = peak.T, total.T
        top = jnp.max(pt, axis=0, keepdims=True)
        out[place(q)] = top + jnp.log(jnp.sum(tt * jnp.exp2(pt - top), axis=0, keepdims=True)) * LOG2E


def spread(sp, col, place):
    for q in range(NB):
        col[pl.ds(q * BLK, BLK), :] = jnp.broadcast_to(sp[place(q)], (BLK, LANES)).T


def column_sum(w, u, col, c, cw):
    u[c] = jnp.exp2(u[c] + col[...])
    rows = 32
    kk = cw // LANES

    def step(t, accs):
        rr = pl.ds(pl.multiple_of(t * rows, rows), rows)
        ut = u[c, rr, :]
        return tuple(
            a + jnp.sum((w[rr, pl.ds(c * cw + k * LANES, LANES)] * ut).reshape(rows // 8, 8, LANES), axis=0)
            for k, a in enumerate(accs)
        )

    zero = tuple(jnp.zeros((8, LANES), jnp.float32) for _ in range(kk))
    accs = lax.fori_loop(0, w.shape[0] // rows, step, zero, unroll=4)
    return jnp.concatenate([jnp.sum(a, axis=0, keepdims=True) for a in accs], axis=1)


def weight_pass(w, gain, tm, ms, c, cw):
    rows = 32
    kk = cw // LANES

    def step(i, _):
        rr = pl.ds(pl.multiple_of(i * rows, rows), rows)
        peak = total = None
        for k in range(kk):
            cols = pl.ds(c * cw + k * LANES, LANES)
            e = w[rr, cols] * gain[:, cols]
            peak = e if peak is None else jnp.maximum(peak, e)
            total = e if total is None else total + e
        tm[c, rr, :] = peak
        ms[c, rr, :] = total
        return 0

    lax.fori_loop(0, w.shape[0] // rows, step, 0, unroll=4)


def block_mass(u, ms, row0):
    rr = pl.ds(row0, BLK)
    return jnp.sum(sum(ms[c, rr, :] * u[c, rr, :] for c in range(NCHUNK)).T, axis=0, keepdims=True)


def block_features(w, u, gain, tm, feat, row0, rows, cw):
    rr = pl.ds(row0, rows)
    peak = functools.reduce(jnp.maximum, [tm[c, rr, :] * u[c, rr, :] for c in range(NCHUNK)])
    peak = jnp.maximum(jnp.max(peak, axis=1, keepdims=True), TINY)
    inv = 1.0 / peak
    weights = []
    for c in range(NCHUNK):
        a = u[c, rr, :] * inv
        for k in range(cw // LANES):
            cols = pl.ds(c * cw + k * LANES, LANES)
            weights.append((w[rr, cols] * a * gain[:, cols]).astype(jnp.bfloat16))
    return jnp.dot(jnp.concatenate(weights, axis=1), feat[...], preferred_element_type=jnp.float32) * peak


def lse_parts(parts):
    top = jnp.max(parts, axis=0)
    return top + jnp.log(jnp.sum(jnp.exp2(parts - top[None]), axis=0)) * LOG2E


def kernel(v_hbm, r_hbm, feat_hbm, sup_hbm, dem_hbm, out,
           v_all, r, feat, sup, dem, z, w, top, acc, d, gain, m, s, tm,
           col, xbuf, zbuf, rowbuf, massown, massbuf, sp, fgive, fkeep, fmate, fsend, frecv,
           load_sem, ag_send, ag_recv, relay, x_send, x_recv, z_send, z_recv, row_sem, mass_sem,
           mate_send, mate_recv, f_send, f_recv):
    me, b = lax.axis_index("veh"), lax.axis_index("req")
    zc, xc = me // NX, lax.rem(me, NX)
    y, core = b // 2, lax.rem(b, 2)
    cw = z.shape[1] // NCHUNK
    scale = 3.0 / math.sqrt(v_hbm.shape[1]) * LOG2E

    def x_peer(k):
        return (zc * NX + lax.rem(xc + k, NX), b)

    def z_peer(k):
        return (lax.rem(zc + k, NZ) * NX + xc, b)

    def req_peer(k):
        return (me, lax.rem(b + k, NB))

    def at(dy, dc):
        return lax.rem(y + dy, NY) * 2 + lax.rem(core + dc, 2)

    def place(q):
        return at(q // 2, q % 2)

    loads = [
        pltpu.make_async_copy(v_hbm, v_all.at[0], load_sem.at[0]),
        pltpu.make_async_copy(r_hbm, r, load_sem.at[1]),
        pltpu.make_async_copy(sup_hbm, sup, load_sem.at[2]),
        pltpu.make_async_copy(dem_hbm, dem, load_sem.at[3]),
        pltpu.make_async_copy(feat_hbm, feat, load_sem.at[4]),
    ]
    sent = []
    loads[0].start()
    barrier = pltpu.get_barrier_semaphore()
    near_z = (z_peer(1), z_peer(NZ - 1))
    for peer in [req_peer(k) for k in range(1, NB)] + [x_peer(k) for k in range(1, NX)] + list(near_z):
        pl.semaphore_signal(barrier, inc=1, device_id=peer, device_id_type=MESH)
    for load in loads[1:4]:
        load.start()
    loads[0].wait()
    pl.semaphore_wait(barrier, NB - 1 + NX - 1 + 2)

    def tell(i):
        for peer in near_z:
            pl.semaphore_signal(relay.at[i], inc=1, device_id=peer, device_id_type=MESH)

    def told(i):
        pl.semaphore_wait(relay.at[i], 2)

    for q in (4, 5, 2, 6, 3, 7, 1):
        dy, dc = q // 2, q % 2
        there = (NY - dy) % NY * 2 + dc
        copy = pltpu.make_async_remote_copy(
            v_all.at[0], v_all.at[there], ag_send.at[q], ag_recv.at[there],
            device_id=(me, at(dy, dc)), device_id_type=MESH)
        copy.start()
        sent.append(copy.wait_send)
    tell(0)

    def arrived(*blocks):
        for q in blocks:
            pltpu.make_async_copy(v_all.at[q], v_all.at[q], ag_recv.at[q]).wait()

    loads[1].wait()
    loads[4].start()
    score_rows(v_all, r, z, top, acc, 0, 1, scale, first=True)
    told(0)
    tell(1)
    arrived(1)
    score_rows(v_all, r, z, top, acc, 1, 1, scale)
    told(1)
    tell(2)
    arrived(2, 3)
    score_rows(v_all, r, z, top, acc, 2, 2, scale)
    told(2)
    arrived(6, 7)
    score_rows(v_all, r, z, top, acc, 6, 2, scale)
    arrived(4, 5)

    def x_start(a, c):
        for k in range(1, NX):
            pltpu.make_async_remote_copy(
                xbuf.at[a, c, NX - 1], xbuf.at[a, c, NX - 1 - k], x_send.at[a, c], x_recv.at[a, c],
                device_id=x_peer(k), device_id_type=MESH).start()
        sent.append(lambda: all_of(xbuf.at[a, c], NX - 1, x_send.at[a, c]))

    def z_start(a, c):
        for k in range(1, NZ):
            pltpu.make_async_remote_copy(
                zbuf.at[a, c, NZ - 1], zbuf.at[a, c, NZ - 1 - k], z_send.at[a, c], z_recv.at[a, c],
                device_id=z_peer(k), device_id_type=MESH).start()
        sent.append(lambda: all_of(zbuf.at[a, c], NZ - 1, z_send.at[a, c]))

    def all_of(buf, n, sem):
        pltpu.make_async_copy(buf.at[pl.ds(0, n)], buf.at[pl.ds(0, n)], sem).wait()

    loads[2].wait()
    loads[3].wait()
    for c in range(NCHUNK):
        score_rows(v_all, r, z, top, acc, 4, 2, scale, start=c * cw, stop=(c + 1) * cw)
        xbuf[0, c, NX - 1] = column_lse(top, acc, pl.ds(c * cw, cw))
        x_start(0, c)
    for c in range(NCHUNK):
        all_of(xbuf.at[0, c], NX - 1, x_recv.at[0, c])
        zbuf[0, c, NZ - 1] = lse_parts(xbuf[0, c])
        z_start(0, c)
    for c in range(NCHUNK):
        all_of(zbuf.at[0, c], NZ - 1, z_recv.at[0, c])
        cols = pl.ds(c * cw, cw)
        d[:, cols] = dem[:, cols] * LOG2E - lse_parts(zbuf[0, c])
        row_pass(z, d, w, m, s, c, cw)

    row_totals(m, s, rowbuf.at[NB - 1], place)
    for k in range(1, NB):
        pltpu.make_async_remote_copy(
            rowbuf.at[NB - 1], rowbuf.at[NB - 1 - k], row_sem.at[0], row_sem.at[1],
            device_id=req_peer(k), device_id_type=MESH).start()
    sent.append(lambda: all_of(rowbuf, NB - 1, row_sem.at[0]))
    all_of(rowbuf, NB - 1, row_sem.at[1])
    sp[...] = sup[...] * LOG2E - lse_parts(rowbuf[...])
    spread(sp, col, place)

    for c in range(NCHUNK):
        xbuf[1, c, NX - 1] = column_sum(w, m, col, c, cw)
        x_start(1, c)
    for c in range(NCHUNK):
        all_of(xbuf.at[1, c], NX - 1, x_recv.at[1, c])
        zbuf[1, c, NZ - 1] = jnp.sum(xbuf[1, c], axis=0)
        z_start(1, c)
    for c in range(NCHUNK):
        all_of(zbuf.at[1, c], NZ - 1, z_recv.at[1, c])
        cols = pl.ds(c * cw, cw)
        gain[:, cols] = jnp.exp2(dem[:, cols] * LOG2E) / jnp.sum(zbuf[1, c], axis=0)
        weight_pass(w, gain, tm, s, c, cw)

    def mate_copy(dy):
        return pltpu.make_async_remote_copy(
            fgive.at[dy], fmate.at[dy], mate_send.at[dy], mate_recv.at[dy],
            device_id=(me, at(0, 1)), device_id_type=MESH)

    def out_copy(dy):
        return pltpu.make_async_remote_copy(
            fsend.at[dy - 1], frecv.at[dy - 1], f_send.at[dy - 1], f_recv.at[dy - 1],
            device_id=(me, at(dy, 0)), device_id_type=MESH)

    def unit(dy):
        f = block_features(w, m, gain, tm, feat, dy * 2 * BLK, 2 * BLK, cw)
        fgive[dy] = f[BLK:]
        mate_copy(dy).start()
        fkeep[dy] = f[:BLK]

    def pass_on(dy):
        mate_copy(dy).wait_recv()
        fsend[dy - 1] = (fkeep[dy] + fmate[dy]).astype(jnp.bfloat16)
        out_copy(dy).start()

    loads[4].wait()
    unit(2)
    unit(1)
    pass_on(2)
    unit(3)
    pass_on(1)
    for q in range(NB):
        massown[q] = block_mass(m, s, q * BLK)
    for q in range(1, NB):
        there = (NY - q // 2) % NY * 2 + q % 2
        pltpu.make_async_remote_copy(
            massown.at[q], massbuf.at[there], mass_sem.at[0], mass_sem.at[1],
            device_id=(me, place(q)), device_id_type=MESH).start()
    others = massbuf.at[pl.ds(1, NB - 1)]
    sent.append(lambda: pltpu.make_async_copy(others, others, mass_sem.at[0]).wait())
    massbuf[0] = massown[0]

    pass_on(3)
    unit(0)
    for wait in sent:
        wait()
    pltpu.make_async_copy(others, others, mass_sem.at[1]).wait()
    mass = jnp.sum(massbuf[...], axis=0)
    inv = 1.0 / jnp.broadcast_to(mass, (BLK, LANES)).T
    mate_copy(0).wait_recv()
    total = fkeep[0] + fmate[0]
    for dy in (1, 2, 3):
        out_copy(dy).wait_recv()
        total = total + frecv[dy - 1].astype(jnp.float32)
    for k in range(feat.shape[1] // LANES):
        out[:, k * LANES:(k + 1) * LANES] = total[:, k * LANES:(k + 1) * LANES] * inv
    for dy in range(NY):
        mate_copy(dy).wait_send()
        if dy:
            out_copy(dy).wait_send()


def local(vehicle_emb, request_emb, request_feat, log_supply, log_demand):
    rows, cols, width = BLK * NB, request_emb.shape[0], request_feat.shape[1]
    cw = cols // NCHUNK
    f32, bf16 = jnp.float32, jnp.bfloat16
    dma = pltpu.SemaphoreType.DMA
    scratch = [
        pltpu.VMEM((NB, BLK, vehicle_emb.shape[1]), bf16),
        pltpu.VMEM(request_emb.shape, bf16),
        pltpu.VMEM(request_feat.shape, bf16),
        pltpu.VMEM((NB, 1, LANES), f32),
        pltpu.VMEM((1, cols), f32),
        pltpu.VMEM((rows, cols), f32),
        pltpu.VMEM((rows, cols), f32),
        pltpu.VMEM((8, cols), f32),
        pltpu.VMEM((8, cols), f32),
        pltpu.VMEM((1, cols), f32),
        pltpu.VMEM((1, cols), f32),
        pltpu.VMEM((NCHUNK, rows, LANES), f32),
        pltpu.VMEM((NCHUNK, rows, LANES), f32),
        pltpu.VMEM((NCHUNK, rows, LANES), f32),
        pltpu.VMEM((rows, LANES), f32),
        pltpu.VMEM((2, NCHUNK, NX, 1, cw), f32),
        pltpu.VMEM((2, NCHUNK, NZ, 1, cw), f32),
        pltpu.VMEM((NB, NB, 1, LANES), f32),
        pltpu.VMEM((NB, 1, LANES), f32),
        pltpu.VMEM((NB, 1, LANES), f32),
        pltpu.VMEM((NB, 1, LANES), f32),
        pltpu.VMEM((NY, BLK, width), f32),
        pltpu.VMEM((NY, BLK, width), f32),
        pltpu.VMEM((NY, BLK, width), f32),
        pltpu.VMEM((NY - 1, BLK, width), bf16),
        pltpu.VMEM((NY - 1, BLK, width), bf16),
        dma((5,)), dma((NB,)), dma((NB,)), pltpu.SemaphoreType.REGULAR((3,)),
        dma((2, NCHUNK)), dma((2, NCHUNK)), dma((2, NCHUNK)), dma((2, NCHUNK)),
        dma((2,)), dma((2,)),
        dma((NY,)), dma((NY,)), dma((NY - 1,)), dma((NY - 1,)),
    ]
    return pl.pallas_call(
        kernel,
        out_shape=pltpu.VMEM((BLK, width), f32),
        in_specs=[pl.BlockSpec(memory_space=pltpu.HBM)] * 5,
        out_specs=pl.BlockSpec(memory_space=pltpu.VMEM),
        scratch_shapes=scratch,
        compiler_params=pltpu.CompilerParams(
            collective_id=0, has_side_effects=True, vmem_limit_bytes=56 * 2**20),
        cost_estimate=pl.CostEstimate(
            flops=2 * rows * cols * (vehicle_emb.shape[1] + width), bytes_accessed=4 * 2**20,
            transcendentals=2 * rows * cols),
        name="sinkhorn_assign",
    )(vehicle_emb, request_emb, request_feat, log_supply.reshape(NB, 1, LANES), log_demand.reshape(1, cols))


def solution(mesh):
    in_specs = (P(("veh", "req"), None), P("req", None), P("req", None), P("veh"), P("req"))
    out_specs = P(("veh", "req"), None)
    return jax.shard_map(local, mesh=mesh, in_specs=in_specs, out_specs=out_specs, check_vma=False)
```

```python
import functools
import math

import jax
import jax.numpy as jnp
from jax import lax
from jax.experimental import pallas as pl
from jax.experimental.pallas import tpu as pltpu
from jax.sharding import PartitionSpec as P

MESH = pl.DeviceIdType.MESH
LOG2E = 1.4426950408889634
NX, NZ, NY = 4, 8, 4
NB = 8
BLK = 128
LANES = 128
NCHUNK = 4
TINY = 1e-30


def score_rows(v_all, r, z, top, acc, slot, n, scale, first=False, start=0, stop=None):
    width = 512
    v = v_all[slot:slot + n].reshape(n * BLK, v_all.shape[2])
    rows = pl.ds(slot * BLK, n * BLK)
    for c in range(start, stop or z.shape[1], width):
        cols = pl.ds(c, width)
        s = lax.dot_general(v, r[cols, :], (((1,), (1,)), ((), ())), preferred_element_type=jnp.float32) * scale
        z[rows, cols] = s
        s = s.reshape(n * BLK // 8, 8, width)
        peak = jnp.max(s, axis=0)
        if not first:
            old = top[:, cols]
            peak = jnp.maximum(old, peak)
        e = jnp.sum(jnp.exp2(s - peak[None]), axis=0)
        top[:, cols] = peak
        acc[:, cols] = e if first else acc[:, cols] * jnp.exp2(old - peak) + e


def column_lse(top, acc, cols):
    t = top[:, cols]
    peak = jnp.max(t, axis=0, keepdims=True)
    return peak + jnp.log(jnp.sum(acc[:, cols] * jnp.exp2(t - peak), axis=0, keepdims=True)) * LOG2E


def row_pass(z, d, w, m, s, c, cw):
    rows = 64
    kk = cw // LANES

    def step(t, _):
        rr = pl.ds(pl.multiple_of(t * rows, rows), rows)
        ys = [z[rr, pl.ds(c * cw + k * LANES, LANES)] + d[:, pl.ds(c * cw + k * LANES, LANES)] for k in range(kk)]
        peak = functools.reduce(jnp.maximum, ys)
        total = None
        for k in range(kk):
            e = jnp.exp2(ys[k] - peak)
            w[rr, pl.ds(c * cw + k * LANES, LANES)] = e
            total = e if total is None else total + e
        m[c, rr, :] = peak
        s[c, rr, :] = total
        return 0

    lax.fori_loop(0, z.shape[0] // rows, step, 0, unroll=2)


def row_totals(m, s, out, place):
    for q in range(NB):
        rr = pl.ds(q * BLK, BLK)
        peak = functools.reduce(jnp.maximum, [m[c, rr, :] for c in range(NCHUNK)])
        total = sum(s[c, rr, :] * jnp.exp2(m[c, rr, :] - peak) for c in range(NCHUNK))
        pt, tt = peak.T, total.T
        top = jnp.max(pt, axis=0, keepdims=True)
        out[place(q)] = top + jnp.log(jnp.sum(tt * jnp.exp2(pt - top), axis=0, keepdims=True)) * LOG2E


def spread(sp, col, place):
    for q in range(NB):
        col[pl.ds(q * BLK, BLK), :] = jnp.broadcast_to(sp[place(q)], (BLK, LANES)).T


def column_sum(w, u, col, c, cw):
    u[c] = jnp.exp2(u[c] + col[...])
    rows = 32
    kk = cw // LANES

    def step(t, accs):
        rr = pl.ds(pl.multiple_of(t * rows, rows), rows)
        ut = u[c, rr, :]
        return tuple(
            a + jnp.sum((w[rr, pl.ds(c * cw + k * LANES, LANES)] * ut).reshape(rows // 8, 8, LANES), axis=0)
            for k, a in enumerate(accs)
        )

    zero = tuple(jnp.zeros((8, LANES), jnp.float32) for _ in range(kk))
    accs = lax.fori_loop(0, w.shape[0] // rows, step, zero, unroll=4)
    return jnp.concatenate([jnp.sum(a, axis=0, keepdims=True) for a in accs], axis=1)


def weight_pass(w, gain, tm, ms, c, cw):
    rows = 32
    kk = cw // LANES

    def step(i, _):
        rr = pl.ds(pl.multiple_of(i * rows, rows), rows)
        peak = total = None
        for k in range(kk):
            cols = pl.ds(c * cw + k * LANES, LANES)
            e = w[rr, cols] * gain[:, cols]
            peak = e if peak is None else jnp.maximum(peak, e)
            total = e if total is None else total + e
        tm[c, rr, :] = peak
        ms[c, rr, :] = total
        return 0

    lax.fori_loop(0, w.shape[0] // rows, step, 0, unroll=4)


def block_mass(u, ms, row0):
    rr = pl.ds(row0, BLK)
    return jnp.sum(sum(ms[c, rr, :] * u[c, rr, :] for c in range(NCHUNK)).T, axis=0, keepdims=True)


def block_features(w, u, gain, tm, feat, row0, rows, cw):
    rr = pl.ds(row0, rows)
    peak = functools.reduce(jnp.maximum, [tm[c, rr, :] * u[c, rr, :] for c in range(NCHUNK)])
    peak = jnp.maximum(jnp.max(peak, axis=1, keepdims=True), TINY)
    inv = 1.0 / peak
    weights = []
    for c in range(NCHUNK):
        a = u[c, rr, :] * inv
        for k in range(cw // LANES):
            cols = pl.ds(c * cw + k * LANES, LANES)
            weights.append((w[rr, cols] * a * gain[:, cols]).astype(jnp.bfloat16))
    return jnp.dot(jnp.concatenate(weights, axis=1), feat[...], preferred_element_type=jnp.float32) * peak


def lse_parts(parts):
    top = jnp.max(parts, axis=0)
    return top + jnp.log(jnp.sum(jnp.exp2(parts - top[None]), axis=0)) * LOG2E


def kernel(v_hbm, r_hbm, feat_hbm, sup_hbm, dem_hbm, out,
           v_all, r, feat, sup, dem, z, w, top, acc, d, gain, m, s, tm,
           col, xbuf, zbuf, rowbuf, massown, massbuf, sp, fgive, fkeep, fmate, fsend, frecv,
           load_sem, ag_send, ag_recv, relay, x_send, x_recv, z_send, z_recv, row_sem, mass_sem,
           mate_send, mate_recv, f_send, f_recv):
    me, b = lax.axis_index("veh"), lax.axis_index("req")
    zc, xc = me // NX, lax.rem(me, NX)
    y, core = b // 2, lax.rem(b, 2)
    cw = z.shape[1] // NCHUNK
    scale = 3.0 / math.sqrt(v_hbm.shape[1]) * LOG2E

    def x_peer(k):
        return (zc * NX + lax.rem(xc + k, NX), b)

    def z_peer(k):
        return (lax.rem(zc + k, NZ) * NX + xc, b)

    def req_peer(k):
        return (me, lax.rem(b + k, NB))

    def at(dy, dc):
        return lax.rem(y + dy, NY) * 2 + lax.rem(core + dc, 2)

    def place(q):
        return at(q // 2, q % 2)

    loads = [
        pltpu.make_async_copy(v_hbm, v_all.at[0], load_sem.at[0]),
        pltpu.make_async_copy(r_hbm, r, load_sem.at[1]),
        pltpu.make_async_copy(sup_hbm, sup, load_sem.at[2]),
        pltpu.make_async_copy(dem_hbm, dem, load_sem.at[3]),
        pltpu.make_async_copy(feat_hbm, feat, load_sem.at[4]),
    ]
    sent = []
    barrier = pltpu.get_barrier_semaphore()
    near_z = (z_peer(1), z_peer(NZ - 1))
    for peer in [req_peer(k) for k in range(1, NB)] + [x_peer(k) for k in range(1, NX)] + list(near_z):
        pl.semaphore_signal(barrier, inc=1, device_id=peer, device_id_type=MESH)
    for load in loads[:4]:
        load.start()
    pl.semaphore_wait(barrier, NB - 1 + NX - 1 + 2)

    def tell(i):
        for peer in near_z:
            pl.semaphore_signal(relay.at[i], inc=1, device_id=peer, device_id_type=MESH)

    def told(i):
        pl.semaphore_wait(relay.at[i], 2)

    for q in (4, 5, 2, 6, 3, 7, 1):
        dy, dc = q // 2, q % 2
        there = (NY - dy) % NY * 2 + dc
        copy = pltpu.make_async_remote_copy(
            v_hbm, v_all.at[there], ag_send.at[q], ag_recv.at[there],
            device_id=(me, at(dy, dc)), device_id_type=MESH)
        copy.start()
        sent.append(copy.wait_send)
    tell(0)

    def arrived(*blocks):
        for q in blocks:
            pltpu.make_async_copy(v_all.at[q], v_all.at[q], ag_recv.at[q]).wait()

    loads[0].wait()
    loads[1].wait()
    loads[4].start()
    score_rows(v_all, r, z, top, acc, 0, 1, scale, first=True)
    told(0)
    tell(1)
    arrived(1)
    score_rows(v_all, r, z, top, acc, 1, 1, scale)
    told(1)
    tell(2)
    arrived(2, 3)
    score_rows(v_all, r, z, top, acc, 2, 2, scale)
    told(2)
    arrived(6, 7)
    score_rows(v_all, r, z, top, acc, 6, 2, scale)
    arrived(4, 5)

    def x_start(a, c):
        for k in (2, 1, 3):
            pltpu.make_async_remote_copy(
                xbuf.at[a, c, NX - 1], xbuf.at[a, c, NX - 1 - k], x_send.at[a, c], x_recv.at[a, c],
                device_id=x_peer(k), device_id_type=MESH).start()
        sent.append(lambda: all_of(xbuf.at[a, c], NX - 1, x_send.at[a, c]))

    def z_start(a, c):
        for k in (4, 3, 5, 2, 6, 1, 7):
            pltpu.make_async_remote_copy(
                zbuf.at[a, c, NZ - 1], zbuf.at[a, c, NZ - 1 - k], z_send.at[a, c], z_recv.at[a, c],
                device_id=z_peer(k), device_id_type=MESH).start()
        sent.append(lambda: all_of(zbuf.at[a, c], NZ - 1, z_send.at[a, c]))

    def all_of(buf, n, sem):
        pltpu.make_async_copy(buf.at[pl.ds(0, n)], buf.at[pl.ds(0, n)], sem).wait()

    loads[2].wait()
    loads[3].wait()
    for c in range(NCHUNK):
        score_rows(v_all, r, z, top, acc, 4, 2, scale, start=c * cw, stop=(c + 1) * cw)
        xbuf[0, c, NX - 1] = column_lse(top, acc, pl.ds(c * cw, cw))
        x_start(0, c)
    for c in range(NCHUNK):
        all_of(xbuf.at[0, c], NX - 1, x_recv.at[0, c])
        zbuf[0, c, NZ - 1] = lse_parts(xbuf[0, c])
        z_start(0, c)
    for c in range(NCHUNK):
        all_of(zbuf.at[0, c], NZ - 1, z_recv.at[0, c])
        cols = pl.ds(c * cw, cw)
        d[:, cols] = dem[:, cols] * LOG2E - lse_parts(zbuf[0, c])
        row_pass(z, d, w, m, s, c, cw)

    row_totals(m, s, rowbuf.at[NB - 1], place)
    for k in (4, 3, 5, 2, 6, 1, 7):
        pltpu.make_async_remote_copy(
            rowbuf.at[NB - 1], rowbuf.at[NB - 1 - k], row_sem.at[0], row_sem.at[1],
            device_id=req_peer(k), device_id_type=MESH).start()
    sent.append(lambda: all_of(rowbuf, NB - 1, row_sem.at[0]))
    all_of(rowbuf, NB - 1, row_sem.at[1])
    sp[...] = sup[...] * LOG2E - lse_parts(rowbuf[...])
    spread(sp, col, place)

    for c in range(NCHUNK):
        xbuf[1, c, NX - 1] = column_sum(w, m, col, c, cw)
        x_start(1, c)
    for c in range(NCHUNK):
        all_of(xbuf.at[1, c], NX - 1, x_recv.at[1, c])
        zbuf[1, c, NZ - 1] = jnp.sum(xbuf[1, c], axis=0)
        z_start(1, c)
    for c in range(NCHUNK):
        all_of(zbuf.at[1, c], NZ - 1, z_recv.at[1, c])
        cols = pl.ds(c * cw, cw)
        gain[:, cols] = jnp.exp2(dem[:, cols] * LOG2E) / jnp.sum(zbuf[1, c], axis=0)
        weight_pass(w, gain, tm, s, c, cw)

    def mate_copy(dy):
        return pltpu.make_async_remote_copy(
            fgive.at[dy], fmate.at[dy], mate_send.at[dy], mate_recv.at[dy],
            device_id=(me, at(0, 1)), device_id_type=MESH)

    def out_copy(dy):
        return pltpu.make_async_remote_copy(
            fsend.at[dy - 1], frecv.at[dy - 1], f_send.at[dy - 1], f_recv.at[dy - 1],
            device_id=(me, at(dy, 0)), device_id_type=MESH)

    def unit(dy):
        f = block_features(w, m, gain, tm, feat, dy * 2 * BLK, 2 * BLK, cw)
        fgive[dy] = f[BLK:]
        mate_copy(dy).start()
        fkeep[dy] = f[:BLK]

    def pass_on(dy):
        mate_copy(dy).wait_recv()
        fsend[dy - 1] = (fkeep[dy] + fmate[dy]).astype(jnp.bfloat16)
        out_copy(dy).start()

    loads[4].wait()
    unit(2)
    unit(1)
    pass_on(2)
    unit(3)
    pass_on(1)
    for q in range(NB):
        massown[q] = block_mass(m, s, q * BLK)
    for q in range(1, NB):
        there = (NY - q // 2) % NY * 2 + q % 2
        pltpu.make_async_remote_copy(
            massown.at[q], massbuf.at[there], mass_sem.at[0], mass_sem.at[1],
            device_id=(me, place(q)), device_id_type=MESH).start()
    others = massbuf.at[pl.ds(1, NB - 1)]
    sent.append(lambda: pltpu.make_async_copy(others, others, mass_sem.at[0]).wait())
    massbuf[0] = massown[0]

    pass_on(3)
    unit(0)
    for wait in sent:
        wait()
    pltpu.make_async_copy(others, others, mass_sem.at[1]).wait()
    mass = jnp.sum(massbuf[...], axis=0)
    inv = 1.0 / jnp.broadcast_to(mass, (BLK, LANES)).T
    mate_copy(0).wait_recv()
    total = fkeep[0] + fmate[0]
    for dy in (1, 2, 3):
        out_copy(dy).wait_recv()
        total = total + frecv[dy - 1].astype(jnp.float32)
    for k in range(feat.shape[1] // LANES):
        out[:, k * LANES:(k + 1) * LANES] = total[:, k * LANES:(k + 1) * LANES] * inv
    for dy in range(NY):
        mate_copy(dy).wait_send()
        if dy:
            out_copy(dy).wait_send()


def local(vehicle_emb, request_emb, request_feat, log_supply, log_demand):
    rows, cols, width = BLK * NB, request_emb.shape[0], request_feat.shape[1]
    cw = cols // NCHUNK
    f32, bf16 = jnp.float32, jnp.bfloat16
    dma = pltpu.SemaphoreType.DMA
    scratch = [
        pltpu.VMEM((NB, BLK, vehicle_emb.shape[1]), bf16),
        pltpu.VMEM(request_emb.shape, bf16),
        pltpu.VMEM(request_feat.shape, bf16),
        pltpu.VMEM((NB, 1, LANES), f32),
        pltpu.VMEM((1, cols), f32),
        pltpu.VMEM((rows, cols), f32),
        pltpu.VMEM((rows, cols), f32),
        pltpu.VMEM((8, cols), f32),
        pltpu.VMEM((8, cols), f32),
        pltpu.VMEM((1, cols), f32),
        pltpu.VMEM((1, cols), f32),
        pltpu.VMEM((NCHUNK, rows, LANES), f32),
        pltpu.VMEM((NCHUNK, rows, LANES), f32),
        pltpu.VMEM((NCHUNK, rows, LANES), f32),
        pltpu.VMEM((rows, LANES), f32),
        pltpu.VMEM((2, NCHUNK, NX, 1, cw), f32),
        pltpu.VMEM((2, NCHUNK, NZ, 1, cw), f32),
        pltpu.VMEM((NB, NB, 1, LANES), f32),
        pltpu.VMEM((NB, 1, LANES), f32),
        pltpu.VMEM((NB, 1, LANES), f32),
        pltpu.VMEM((NB, 1, LANES), f32),
        pltpu.VMEM((NY, BLK, width), f32),
        pltpu.VMEM((NY, BLK, width), f32),
        pltpu.VMEM((NY, BLK, width), f32),
        pltpu.VMEM((NY - 1, BLK, width), bf16),
        pltpu.VMEM((NY - 1, BLK, width), bf16),
        dma((5,)), dma((NB,)), dma((NB,)), pltpu.SemaphoreType.REGULAR((3,)),
        dma((2, NCHUNK)), dma((2, NCHUNK)), dma((2, NCHUNK)), dma((2, NCHUNK)),
        dma((2,)), dma((2,)),
        dma((NY,)), dma((NY,)), dma((NY - 1,)), dma((NY - 1,)),
    ]
    return pl.pallas_call(
        kernel,
        out_shape=pltpu.VMEM((BLK, width), f32),
        in_specs=[pl.BlockSpec(memory_space=pltpu.HBM)] * 5,
        out_specs=pl.BlockSpec(memory_space=pltpu.VMEM),
        scratch_shapes=scratch,
        compiler_params=pltpu.CompilerParams(
            collective_id=0, has_side_effects=True, vmem_limit_bytes=56 * 2**20),
        cost_estimate=pl.CostEstimate(
            flops=2 * rows * cols * (vehicle_emb.shape[1] + width), bytes_accessed=4 * 2**20,
            transcendentals=2 * rows * cols),
        name="sinkhorn_assign",
    )(vehicle_emb, request_emb, request_feat, log_supply.reshape(NB, 1, LANES), log_demand.reshape(1, cols))


def solution(mesh):
    in_specs = (P(("veh", "req"), None), P("req", None), P("req", None), P("veh"), P("req"))
    out_specs = P(("veh", "req"), None)
    return jax.shard_map(local, mesh=mesh, in_specs=in_specs, out_specs=out_specs, check_vma=False)
```

```python
import functools
import math

import jax
import jax.numpy as jnp
from jax import lax
from jax.experimental import pallas as pl
from jax.experimental.pallas import tpu as pltpu
from jax.sharding import PartitionSpec as P

MESH = pl.DeviceIdType.MESH
LOG2E = 1.4426950408889634
NX, NZ, NY = 4, 8, 4
NB = 8
BLK = 128
LANES = 128
NCHUNK = 4
TINY = 1e-30


def score_rows(v_all, r, z, top, acc, slot, n, scale, first=False, start=0, stop=None):
    width = 512
    v = v_all[slot:slot + n].reshape(n * BLK, v_all.shape[2])
    rows = pl.ds(slot * BLK, n * BLK)
    for c in range(start, stop or z.shape[1], width):
        cols = pl.ds(c, width)
        s = lax.dot_general(v, r[cols, :], (((1,), (1,)), ((), ())), preferred_element_type=jnp.float32) * scale
        z[rows, cols] = s
        s = s.reshape(n * BLK // 8, 8, width)
        peak = jnp.max(s, axis=0)
        if not first:
            old = top[:, cols]
            peak = jnp.maximum(old, peak)
        e = jnp.sum(jnp.exp2(s - peak[None]), axis=0)
        top[:, cols] = peak
        acc[:, cols] = e if first else acc[:, cols] * jnp.exp2(old - peak) + e


def column_lse(top, acc, cols):
    t = top[:, cols]
    peak = jnp.max(t, axis=0, keepdims=True)
    return peak + jnp.log(jnp.sum(acc[:, cols] * jnp.exp2(t - peak), axis=0, keepdims=True)) * LOG2E


def row_pass(z, d, w, m, s, c, cw):
    rows = 64
    kk = cw // LANES

    def step(t, _):
        rr = pl.ds(pl.multiple_of(t * rows, rows), rows)
        ys = [z[rr, pl.ds(c * cw + k * LANES, LANES)] + d[:, pl.ds(c * cw + k * LANES, LANES)] for k in range(kk)]
        peak = functools.reduce(jnp.maximum, ys)
        total = None
        for k in range(kk):
            e = jnp.exp2(ys[k] - peak)
            w[rr, pl.ds(c * cw + k * LANES, LANES)] = e
            total = e if total is None else total + e
        m[c, rr, :] = peak
        s[c, rr, :] = total
        return 0

    lax.fori_loop(0, z.shape[0] // rows, step, 0, unroll=2)


def row_totals(m, s, out, place):
    for q in range(NB):
        rr = pl.ds(q * BLK, BLK)
        peak = functools.reduce(jnp.maximum, [m[c, rr, :] for c in range(NCHUNK)])
        total = sum(s[c, rr, :] * jnp.exp2(m[c, rr, :] - peak) for c in range(NCHUNK))
        pt, tt = peak.T, total.T
        top = jnp.max(pt, axis=0, keepdims=True)
        out[place(q)] = top + jnp.log(jnp.sum(tt * jnp.exp2(pt - top), axis=0, keepdims=True)) * LOG2E


def spread(sp, col, place):
    for q in range(NB):
        col[pl.ds(q * BLK, BLK), :] = jnp.broadcast_to(sp[place(q)], (BLK, LANES)).T


def column_sum(w, u, col, c, cw):
    u[c] = jnp.exp2(u[c] + col[...])
    rows = 32
    kk = cw // LANES

    def step(t, accs):
        rr = pl.ds(pl.multiple_of(t * rows, rows), rows)
        ut = u[c, rr, :]
        return tuple(
            a + jnp.sum((w[rr, pl.ds(c * cw + k * LANES, LANES)] * ut).reshape(rows // 8, 8, LANES), axis=0)
            for k, a in enumerate(accs)
        )

    zero = tuple(jnp.zeros((8, LANES), jnp.float32) for _ in range(kk))
    accs = lax.fori_loop(0, w.shape[0] // rows, step, zero, unroll=4)
    return jnp.concatenate([jnp.sum(a, axis=0, keepdims=True) for a in accs], axis=1)


def weight_pass(w, gain, tm, ms, c, cw):
    rows = 32
    kk = cw // LANES

    def step(i, _):
        rr = pl.ds(pl.multiple_of(i * rows, rows), rows)
        peak = total = None
        for k in range(kk):
            cols = pl.ds(c * cw + k * LANES, LANES)
            e = w[rr, cols] * gain[:, cols]
            peak = e if peak is None else jnp.maximum(peak, e)
            total = e if total is None else total + e
        tm[c, rr, :] = peak
        ms[c, rr, :] = total
        return 0

    lax.fori_loop(0, w.shape[0] // rows, step, 0, unroll=4)


def block_mass(u, ms, row0):
    rr = pl.ds(row0, BLK)
    return jnp.sum(sum(ms[c, rr, :] * u[c, rr, :] for c in range(NCHUNK)).T, axis=0, keepdims=True)


def block_features(w, u, gain, tm, feat, row0, rows, cw):
    rr = pl.ds(row0, rows)
    peak = functools.reduce(jnp.maximum, [tm[c, rr, :] * u[c, rr, :] for c in range(NCHUNK)])
    peak = jnp.maximum(jnp.max(peak, axis=1, keepdims=True), TINY)
    inv = 1.0 / peak
    weights = []
    for c in range(NCHUNK):
        a = u[c, rr, :] * inv
        for k in range(cw // LANES):
            cols = pl.ds(c * cw + k * LANES, LANES)
            weights.append((w[rr, cols] * a * gain[:, cols]).astype(jnp.bfloat16))
    return jnp.dot(jnp.concatenate(weights, axis=1), feat[...], preferred_element_type=jnp.float32) * peak


def lse_parts(parts):
    top = jnp.max(parts, axis=0)
    return top + jnp.log(jnp.sum(jnp.exp2(parts - top[None]), axis=0)) * LOG2E


def kernel(v_hbm, r_hbm, feat_hbm, sup_hbm, dem_hbm, out,
           v_all, r, feat, sup, dem, z, w, top, acc, d, gain, m, s, tm,
           col, xbuf, zbuf, rowbuf, massown, massbuf, sp, fgive, fkeep, fmate, fsend, frecv,
           load_sem, ag_send, ag_recv, relay, x_send, x_recv, z_send, z_recv, row_sem, mass_sem,
           mate_send, mate_recv, f_send, f_recv):
    me, b = lax.axis_index("veh"), lax.axis_index("req")
    zc, xc = me // NX, lax.rem(me, NX)
    y, core = b // 2, lax.rem(b, 2)
    cw = z.shape[1] // NCHUNK
    scale = 3.0 / math.sqrt(v_hbm.shape[1]) * LOG2E

    def x_peer(k):
        return (zc * NX + lax.rem(xc + k, NX), b)

    def z_peer(k):
        return (lax.rem(zc + k, NZ) * NX + xc, b)

    def req_peer(k):
        return (me, lax.rem(b + k, NB))

    def at(dy, dc):
        return lax.rem(y + dy, NY) * 2 + lax.rem(core + dc, 2)

    def place(q):
        return at(q // 2, q % 2)

    loads = [
        pltpu.make_async_copy(v_hbm, v_all.at[0], load_sem.at[0]),
        pltpu.make_async_copy(r_hbm, r, load_sem.at[1]),
        pltpu.make_async_copy(sup_hbm, sup, load_sem.at[2]),
        pltpu.make_async_copy(dem_hbm, dem, load_sem.at[3]),
        pltpu.make_async_copy(feat_hbm, feat, load_sem.at[4]),
    ]
    sent = []
    barrier = pltpu.get_barrier_semaphore()
    near_z = (z_peer(1), z_peer(NZ - 1))
    for peer in [req_peer(k) for k in range(1, NB)] + [x_peer(k) for k in range(1, NX)] + list(near_z):
        pl.semaphore_signal(barrier, inc=1, device_id=peer, device_id_type=MESH)
    for load in loads[:4]:
        load.start()
    pl.semaphore_wait(barrier, NB - 1 + NX - 1 + 2)

    def tell(i):
        for peer in near_z:
            pl.semaphore_signal(relay.at[i], inc=1, device_id=peer, device_id_type=MESH)

    def told(i):
        pl.semaphore_wait(relay.at[i], 2)

    for q in (1, 2, 3, 4, 5, 6, 7):
        dy, dc = q // 2, q % 2
        there = (NY - dy) % NY * 2 + dc
        copy = pltpu.make_async_remote_copy(
            v_hbm, v_all.at[there], ag_send.at[q], ag_recv.at[there],
            device_id=(me, at(dy, dc)), device_id_type=MESH)
        copy.start()
        sent.append(copy.wait_send)
    tell(0)

    def arrived(*blocks):
        for q in blocks:
            pltpu.make_async_copy(v_all.at[q], v_all.at[q], ag_recv.at[q]).wait()

    loads[0].wait()
    loads[1].wait()
    loads[4].start()
    score_rows(v_all, r, z, top, acc, 0, 1, scale, first=True)
    told(0)
    tell(1)
    arrived(1)
    score_rows(v_all, r, z, top, acc, 1, 1, scale)
    told(1)
    tell(2)
    arrived(2, 3)
    score_rows(v_all, r, z, top, acc, 2, 2, scale)
    told(2)
    arrived(4, 5, 6, 7)

    def x_start(a, c):
        for k in (2, 1, 3):
            pltpu.make_async_remote_copy(
                xbuf.at[a, c, NX - 1], xbuf.at[a, c, NX - 1 - k], x_send.at[a, c], x_recv.at[a, c],
                device_id=x_peer(k), device_id_type=MESH).start()
        sent.append(lambda: all_of(xbuf.at[a, c], NX - 1, x_send.at[a, c]))

    def z_start(a, c):
        for k in (4, 3, 5, 2, 6, 1, 7):
            pltpu.make_async_remote_copy(
                zbuf.at[a, c, NZ - 1], zbuf.at[a, c, NZ - 1 - k], z_send.at[a, c], z_recv.at[a, c],
                device_id=z_peer(k), device_id_type=MESH).start()
        sent.append(lambda: all_of(zbuf.at[a, c], NZ - 1, z_send.at[a, c]))

    def all_of(buf, n, sem):
        pltpu.make_async_copy(buf.at[pl.ds(0, n)], buf.at[pl.ds(0, n)], sem).wait()

    loads[2].wait()
    loads[3].wait()
    for c in range(NCHUNK):
        score_rows(v_all, r, z, top, acc, 4, 4, scale, start=c * cw, stop=(c + 1) * cw)
        xbuf[0, c, NX - 1] = column_lse(top, acc, pl.ds(c * cw, cw))
        x_start(0, c)
    for c in range(NCHUNK):
        all_of(xbuf.at[0, c], NX - 1, x_recv.at[0, c])
        zbuf[0, c, NZ - 1] = lse_parts(xbuf[0, c])
        z_start(0, c)
    for c in range(NCHUNK):
        all_of(zbuf.at[0, c], NZ - 1, z_recv.at[0, c])
        cols = pl.ds(c * cw, cw)
        d[:, cols] = dem[:, cols] * LOG2E - lse_parts(zbuf[0, c])
        row_pass(z, d, w, m, s, c, cw)

    row_totals(m, s, rowbuf.at[NB - 1], place)
    for k in (4, 3, 5, 2, 6, 1, 7):
        pltpu.make_async_remote_copy(
            rowbuf.at[NB - 1], rowbuf.at[NB - 1 - k], row_sem.at[0], row_sem.at[1],
            device_id=req_peer(k), device_id_type=MESH).start()
    sent.append(lambda: all_of(rowbuf, NB - 1, row_sem.at[0]))
    all_of(rowbuf, NB - 1, row_sem.at[1])
    sp[...] = sup[...] * LOG2E - lse_parts(rowbuf[...])
    spread(sp, col, place)

    for c in range(NCHUNK):
        xbuf[1, c, NX - 1] = column_sum(w, m, col, c, cw)
        x_start(1, c)
    for c in range(NCHUNK):
        all_of(xbuf.at[1, c], NX - 1, x_recv.at[1, c])
        zbuf[1, c, NZ - 1] = jnp.sum(xbuf[1, c], axis=0)
        z_start(1, c)
    for c in range(NCHUNK):
        all_of(zbuf.at[1, c], NZ - 1, z_recv.at[1, c])
        cols = pl.ds(c * cw, cw)
        gain[:, cols] = jnp.exp2(dem[:, cols] * LOG2E) / jnp.sum(zbuf[1, c], axis=0)
        weight_pass(w, gain, tm, s, c, cw)

    def mate_copy(dy):
        return pltpu.make_async_remote_copy(
            fgive.at[dy], fmate.at[dy], mate_send.at[dy], mate_recv.at[dy],
            device_id=(me, at(0, 1)), device_id_type=MESH)

    def out_copy(dy):
        return pltpu.make_async_remote_copy(
            fsend.at[dy - 1], frecv.at[dy - 1], f_send.at[dy - 1], f_recv.at[dy - 1],
            device_id=(me, at(dy, 0)), device_id_type=MESH)

    def unit(dy):
        f = block_features(w, m, gain, tm, feat, dy * 2 * BLK, 2 * BLK, cw)
        fgive[dy] = f[BLK:]
        mate_copy(dy).start()
        fkeep[dy] = f[:BLK]

    def pass_on(dy):
        mate_copy(dy).wait_recv()
        fsend[dy - 1] = (fkeep[dy] + fmate[dy]).astype(jnp.bfloat16)
        out_copy(dy).start()

    loads[4].wait()
    unit(2)
    unit(1)
    pass_on(2)
    unit(3)
    pass_on(1)
    for q in range(NB):
        massown[q] = block_mass(m, s, q * BLK)
    for q in range(1, NB):
        there = (NY - q // 2) % NY * 2 + q % 2
        pltpu.make_async_remote_copy(
            massown.at[q], massbuf.at[there], mass_sem.at[0], mass_sem.at[1],
            device_id=(me, place(q)), device_id_type=MESH).start()
    others = massbuf.at[pl.ds(1, NB - 1)]
    sent.append(lambda: pltpu.make_async_copy(others, others, mass_sem.at[0]).wait())
    massbuf[0] = massown[0]

    pass_on(3)
    unit(0)
    for wait in sent:
        wait()
    pltpu.make_async_copy(others, others, mass_sem.at[1]).wait()
    mass = jnp.sum(massbuf[...], axis=0)
    inv = 1.0 / jnp.broadcast_to(mass, (BLK, LANES)).T
    mate_copy(0).wait_recv()
    total = fkeep[0] + fmate[0]
    for dy in (1, 2, 3):
        out_copy(dy).wait_recv()
        total = total + frecv[dy - 1].astype(jnp.float32)
    for k in range(feat.shape[1] // LANES):
        out[:, k * LANES:(k + 1) * LANES] = total[:, k * LANES:(k + 1) * LANES] * inv
    for dy in range(NY):
        mate_copy(dy).wait_send()
        if dy:
            out_copy(dy).wait_send()


def local(vehicle_emb, request_emb, request_feat, log_supply, log_demand):
    rows, cols, width = BLK * NB, request_emb.shape[0], request_feat.shape[1]
    cw = cols // NCHUNK
    f32, bf16 = jnp.float32, jnp.bfloat16
    dma = pltpu.SemaphoreType.DMA
    scratch = [
        pltpu.VMEM((NB, BLK, vehicle_emb.shape[1]), bf16),
        pltpu.VMEM(request_emb.shape, bf16),
        pltpu.VMEM(request_feat.shape, bf16),
        pltpu.VMEM((NB, 1, LANES), f32),
        pltpu.VMEM((1, cols), f32),
        pltpu.VMEM((rows, cols), f32),
        pltpu.VMEM((rows, cols), f32),
        pltpu.VMEM((8, cols), f32),
        pltpu.VMEM((8, cols), f32),
        pltpu.VMEM((1, cols), f32),
        pltpu.VMEM((1, cols), f32),
        pltpu.VMEM((NCHUNK, rows, LANES), f32),
        pltpu.VMEM((NCHUNK, rows, LANES), f32),
        pltpu.VMEM((NCHUNK, rows, LANES), f32),
        pltpu.VMEM((rows, LANES), f32),
        pltpu.VMEM((2, NCHUNK, NX, 1, cw), f32),
        pltpu.VMEM((2, NCHUNK, NZ, 1, cw), f32),
        pltpu.VMEM((NB, NB, 1, LANES), f32),
        pltpu.VMEM((NB, 1, LANES), f32),
        pltpu.VMEM((NB, 1, LANES), f32),
        pltpu.VMEM((NB, 1, LANES), f32),
        pltpu.VMEM((NY, BLK, width), f32),
        pltpu.VMEM((NY, BLK, width), f32),
        pltpu.VMEM((NY, BLK, width), f32),
        pltpu.VMEM((NY - 1, BLK, width), bf16),
        pltpu.VMEM((NY - 1, BLK, width), bf16),
        dma((5,)), dma((NB,)), dma((NB,)), pltpu.SemaphoreType.REGULAR((3,)),
        dma((2, NCHUNK)), dma((2, NCHUNK)), dma((2, NCHUNK)), dma((2, NCHUNK)),
        dma((2,)), dma((2,)),
        dma((NY,)), dma((NY,)), dma((NY - 1,)), dma((NY - 1,)),
    ]
    return pl.pallas_call(
        kernel,
        out_shape=pltpu.VMEM((BLK, width), f32),
        in_specs=[pl.BlockSpec(memory_space=pltpu.HBM)] * 5,
        out_specs=pl.BlockSpec(memory_space=pltpu.VMEM),
        scratch_shapes=scratch,
        compiler_params=pltpu.CompilerParams(
            collective_id=0, has_side_effects=True, vmem_limit_bytes=56 * 2**20),
        cost_estimate=pl.CostEstimate(
            flops=2 * rows * cols * (vehicle_emb.shape[1] + width), bytes_accessed=4 * 2**20,
            transcendentals=2 * rows * cols),
        name="sinkhorn_assign",
    )(vehicle_emb, request_emb, request_feat, log_supply.reshape(NB, 1, LANES), log_demand.reshape(1, cols))


def solution(mesh):
    in_specs = (P(("veh", "req"), None), P("req", None), P("req", None), P("veh"), P("req"))
    out_specs = P(("veh", "req"), None)
    return jax.shard_map(local, mesh=mesh, in_specs=in_specs, out_specs=out_specs, check_vma=False)
```

```python
import functools
import math

import jax
import jax.numpy as jnp
from jax import lax
from jax.experimental import pallas as pl
from jax.experimental.pallas import tpu as pltpu
from jax.sharding import PartitionSpec as P

MESH = pl.DeviceIdType.MESH
LOG2E = 1.4426950408889634
NX, NZ, NY = 4, 8, 4
NB = 8
BLK = 128
LANES = 128
NCHUNK = 4
TINY = 1e-30


def score_rows(v_all, r, z, top, acc, slot, n, scale, first=False, start=0, stop=None):
    width = 512
    v = v_all[slot:slot + n].reshape(n * BLK, v_all.shape[2])
    rows = pl.ds(slot * BLK, n * BLK)
    for c in range(start, stop or z.shape[1], width):
        cols = pl.ds(c, width)
        s = lax.dot_general(v, r[cols, :], (((1,), (1,)), ((), ())), preferred_element_type=jnp.float32) * scale
        z[rows, cols] = s
        s = s.reshape(n * BLK // 8, 8, width)
        peak = jnp.max(s, axis=0)
        if not first:
            old = top[:, cols]
            peak = jnp.maximum(old, peak)
        e = jnp.sum(jnp.exp2(s - peak[None]), axis=0)
        top[:, cols] = peak
        acc[:, cols] = e if first else acc[:, cols] * jnp.exp2(old - peak) + e


def column_lse(top, acc, cols):
    t = top[:, cols]
    peak = jnp.max(t, axis=0, keepdims=True)
    return peak + jnp.log(jnp.sum(acc[:, cols] * jnp.exp2(t - peak), axis=0, keepdims=True)) * LOG2E


def row_pass(z, d, w, m, s, c, cw):
    rows = 64
    kk = cw // LANES

    def step(t, _):
        rr = pl.ds(pl.multiple_of(t * rows, rows), rows)
        ys = [z[rr, pl.ds(c * cw + k * LANES, LANES)] + d[:, pl.ds(c * cw + k * LANES, LANES)] for k in range(kk)]
        peak = functools.reduce(jnp.maximum, ys)
        total = None
        for k in range(kk):
            e = jnp.exp2(ys[k] - peak)
            w[rr, pl.ds(c * cw + k * LANES, LANES)] = e
            total = e if total is None else total + e
        m[c, rr, :] = peak
        s[c, rr, :] = total
        return 0

    lax.fori_loop(0, z.shape[0] // rows, step, 0, unroll=2)


def row_totals(m, s, out, place):
    for q in range(NB):
        rr = pl.ds(q * BLK, BLK)
        peak = functools.reduce(jnp.maximum, [m[c, rr, :] for c in range(NCHUNK)])
        total = sum(s[c, rr, :] * jnp.exp2(m[c, rr, :] - peak) for c in range(NCHUNK))
        pt, tt = peak.T, total.T
        top = jnp.max(pt, axis=0, keepdims=True)
        out[place(q)] = top + jnp.log(jnp.sum(tt * jnp.exp2(pt - top), axis=0, keepdims=True)) * LOG2E


def spread(sp, col, place):
    for q in range(NB):
        col[pl.ds(q * BLK, BLK), :] = jnp.broadcast_to(sp[place(q)], (BLK, LANES)).T


def column_sum(w, u, col, c, cw):
    u[c] = jnp.exp2(u[c] + col[...])
    rows = 32
    kk = cw // LANES

    def step(t, accs):
        rr = pl.ds(pl.multiple_of(t * rows, rows), rows)
        ut = u[c, rr, :]
        return tuple(
            a + jnp.sum((w[rr, pl.ds(c * cw + k * LANES, LANES)] * ut).reshape(rows // 8, 8, LANES), axis=0)
            for k, a in enumerate(accs)
        )

    zero = tuple(jnp.zeros((8, LANES), jnp.float32) for _ in range(kk))
    accs = lax.fori_loop(0, w.shape[0] // rows, step, zero, unroll=4)
    return jnp.concatenate([jnp.sum(a, axis=0, keepdims=True) for a in accs], axis=1)


def weight_pass(w, gain, tm, ms, c, cw):
    rows = 32
    kk = cw // LANES

    def step(i, _):
        rr = pl.ds(pl.multiple_of(i * rows, rows), rows)
        peak = total = None
        for k in range(kk):
            cols = pl.ds(c * cw + k * LANES, LANES)
            e = w[rr, cols] * gain[:, cols]
            peak = e if peak is None else jnp.maximum(peak, e)
            total = e if total is None else total + e
        tm[c, rr, :] = peak
        ms[c, rr, :] = total
        return 0

    lax.fori_loop(0, w.shape[0] // rows, step, 0, unroll=4)


def block_mass(u, ms, row0):
    rr = pl.ds(row0, BLK)
    return jnp.sum(sum(ms[c, rr, :] * u[c, rr, :] for c in range(NCHUNK)).T, axis=0, keepdims=True)


def block_features(w, u, gain, tm, feat, row0, rows, cw):
    rr = pl.ds(row0, rows)
    peak = functools.reduce(jnp.maximum, [tm[c, rr, :] * u[c, rr, :] for c in range(NCHUNK)])
    peak = jnp.maximum(jnp.max(peak, axis=1, keepdims=True), TINY)
    inv = 1.0 / peak
    weights = []
    for c in range(NCHUNK):
        a = u[c, rr, :] * inv
        for k in range(cw // LANES):
            cols = pl.ds(c * cw + k * LANES, LANES)
            weights.append((w[rr, cols] * a * gain[:, cols]).astype(jnp.bfloat16))
    return jnp.dot(jnp.concatenate(weights, axis=1), feat[...], preferred_element_type=jnp.float32) * peak


def lse_parts(parts):
    top = jnp.max(parts, axis=0)
    return top + jnp.log(jnp.sum(jnp.exp2(parts - top[None]), axis=0)) * LOG2E


def kernel(v_hbm, r_hbm, feat_hbm, sup_hbm, dem_hbm, out,
           v_all, r, feat, sup, dem, z, w, top, acc, d, gain, m, s, tm,
           col, xbuf, zbuf, rowbuf, massown, massbuf, sp, fgive, fkeep, fmate, fsend, frecv,
           load_sem, ag_send, ag_recv, relay, x_send, x_recv, z_send, z_recv, row_sem, mass_sem,
           mate_send, mate_recv, f_send, f_recv):
    me, b = lax.axis_index("veh"), lax.axis_index("req")
    zc, xc = me // NX, lax.rem(me, NX)
    y, core = b // 2, lax.rem(b, 2)
    cw = z.shape[1] // NCHUNK
    scale = 3.0 / math.sqrt(v_hbm.shape[1]) * LOG2E

    def x_peer(k):
        return (zc * NX + lax.rem(xc + k, NX), b)

    def z_peer(k):
        return (lax.rem(zc + k, NZ) * NX + xc, b)

    def req_peer(k):
        return (me, lax.rem(b + k, NB))

    def at(dy, dc):
        return lax.rem(y + dy, NY) * 2 + lax.rem(core + dc, 2)

    def place(q):
        return at(q // 2, q % 2)

    loads = [
        pltpu.make_async_copy(v_hbm, v_all.at[0], load_sem.at[0]),
        pltpu.make_async_copy(r_hbm.at[pl.ds(0, cw)], r.at[pl.ds(0, cw)], load_sem.at[1]),
        pltpu.make_async_copy(sup_hbm, sup, load_sem.at[2]),
        pltpu.make_async_copy(dem_hbm, dem, load_sem.at[3]),
        pltpu.make_async_copy(feat_hbm, feat, load_sem.at[4]),
    ]
    sent = []
    barrier = pltpu.get_barrier_semaphore()
    near_z = (z_peer(1), z_peer(NZ - 1))
    for peer in [req_peer(k) for k in range(1, NB)] + [x_peer(k) for k in range(1, NX)] + list(near_z):
        pl.semaphore_signal(barrier, inc=1, device_id=peer, device_id_type=MESH)
    more = [
        pltpu.make_async_copy(r_hbm.at[pl.ds(c * cw, cw)], r.at[pl.ds(c * cw, cw)], load_sem.at[4 + c])
        for c in range(1, NCHUNK)
    ]
    for load in loads[:2] + more + loads[2:4]:
        load.start()
    pl.semaphore_wait(barrier, NB - 1 + NX - 1 + 2)

    def tell(i):
        for peer in near_z:
            pl.semaphore_signal(relay.at[i], inc=1, device_id=peer, device_id_type=MESH)

    def told(i):
        pl.semaphore_wait(relay.at[i], 2)

    for q in (1, 2, 3, 4, 5, 6, 7):
        dy, dc = q // 2, q % 2
        there = (NY - dy) % NY * 2 + dc
        copy = pltpu.make_async_remote_copy(
            v_hbm, v_all.at[there], ag_send.at[q], ag_recv.at[there],
            device_id=(me, at(dy, dc)), device_id_type=MESH)
        copy.start()
        sent.append(copy.wait_send)
    tell(0)

    def arrived(*blocks):
        for q in blocks:
            pltpu.make_async_copy(v_all.at[q], v_all.at[q], ag_recv.at[q]).wait()

    loads[0].wait()
    for c, load in enumerate([loads[1]] + more):
        load.wait()
        score_rows(v_all, r, z, top, acc, 0, 1, scale, first=True, start=c * cw, stop=(c + 1) * cw)
    loads[4].start()
    told(0)
    tell(1)
    arrived(1)
    score_rows(v_all, r, z, top, acc, 1, 1, scale)
    told(1)
    tell(2)
    arrived(2, 3)
    score_rows(v_all, r, z, top, acc, 2, 2, scale)
    told(2)
    arrived(4, 5, 6, 7)

    def x_start(a, c):
        for k in (2, 1, 3):
            pltpu.make_async_remote_copy(
                xbuf.at[a, c, NX - 1], xbuf.at[a, c, NX - 1 - k], x_send.at[a, c], x_recv.at[a, c],
                device_id=x_peer(k), device_id_type=MESH).start()
        sent.append(lambda: all_of(xbuf.at[a, c], NX - 1, x_send.at[a, c]))

    def z_start(a, c):
        for k in (4, 3, 5, 2, 6, 1, 7):
            pltpu.make_async_remote_copy(
                zbuf.at[a, c, NZ - 1], zbuf.at[a, c, NZ - 1 - k], z_send.at[a, c], z_recv.at[a, c],
                device_id=z_peer(k), device_id_type=MESH).start()
        sent.append(lambda: all_of(zbuf.at[a, c], NZ - 1, z_send.at[a, c]))

    def all_of(buf, n, sem):
        pltpu.make_async_copy(buf.at[pl.ds(0, n)], buf.at[pl.ds(0, n)], sem).wait()

    loads[2].wait()
    loads[3].wait()
    for c in range(NCHUNK):
        score_rows(v_all, r, z, top, acc, 4, 4, scale, start=c * cw, stop=(c + 1) * cw)
        xbuf[0, c, NX - 1] = column_lse(top, acc, pl.ds(c * cw, cw))
        x_start(0, c)
    for c in range(NCHUNK):
        all_of(xbuf.at[0, c], NX - 1, x_recv.at[0, c])
        zbuf[0, c, NZ - 1] = lse_parts(xbuf[0, c])
        z_start(0, c)
    for c in range(NCHUNK):
        all_of(zbuf.at[0, c], NZ - 1, z_recv.at[0, c])
        cols = pl.ds(c * cw, cw)
        d[:, cols] = dem[:, cols] * LOG2E - lse_parts(zbuf[0, c])
        row_pass(z, d, w, m, s, c, cw)

    row_totals(m, s, rowbuf.at[NB - 1], place)
    for k in (4, 3, 5, 2, 6, 1, 7):
        pltpu.make_async_remote_copy(
            rowbuf.at[NB - 1], rowbuf.at[NB - 1 - k], row_sem.at[0], row_sem.at[1],
            device_id=req_peer(k), device_id_type=MESH).start()
    sent.append(lambda: all_of(rowbuf, NB - 1, row_sem.at[0]))
    all_of(rowbuf, NB - 1, row_sem.at[1])
    sp[...] = sup[...] * LOG2E - lse_parts(rowbuf[...])
    spread(sp, col, place)

    for c in range(NCHUNK):
        xbuf[1, c, NX - 1] = column_sum(w, m, col, c, cw)
        x_start(1, c)
    for c in range(NCHUNK):
        all_of(xbuf.at[1, c], NX - 1, x_recv.at[1, c])
        zbuf[1, c, NZ - 1] = jnp.sum(xbuf[1, c], axis=0)
        z_start(1, c)
    for c in range(NCHUNK):
        all_of(zbuf.at[1, c], NZ - 1, z_recv.at[1, c])
        cols = pl.ds(c * cw, cw)
        gain[:, cols] = jnp.exp2(dem[:, cols] * LOG2E) / jnp.sum(zbuf[1, c], axis=0)
        weight_pass(w, gain, tm, s, c, cw)

    def mate_copy(dy):
        return pltpu.make_async_remote_copy(
            fgive.at[dy], fmate.at[dy], mate_send.at[dy], mate_recv.at[dy],
            device_id=(me, at(0, 1)), device_id_type=MESH)

    def out_copy(dy):
        return pltpu.make_async_remote_copy(
            fsend.at[dy - 1], frecv.at[dy - 1], f_send.at[dy - 1], f_recv.at[dy - 1],
            device_id=(me, at(dy, 0)), device_id_type=MESH)

    def unit(dy):
        f = block_features(w, m, gain, tm, feat, dy * 2 * BLK, 2 * BLK, cw)
        fgive[dy] = f[BLK:]
        mate_copy(dy).start()
        fkeep[dy] = f[:BLK]

    def pass_on(dy):
        mate_copy(dy).wait_recv()
        fsend[dy - 1] = (fkeep[dy] + fmate[dy]).astype(jnp.bfloat16)
        out_copy(dy).start()

    loads[4].wait()
    unit(2)
    unit(1)
    pass_on(2)
    unit(3)
    pass_on(1)
    for q in range(NB):
        massown[q] = block_mass(m, s, q * BLK)
    for q in range(1, NB):
        there = (NY - q // 2) % NY * 2 + q % 2
        pltpu.make_async_remote_copy(
            massown.at[q], massbuf.at[there], mass_sem.at[0], mass_sem.at[1],
            device_id=(me, place(q)), device_id_type=MESH).start()
    others = massbuf.at[pl.ds(1, NB - 1)]
    sent.append(lambda: pltpu.make_async_copy(others, others, mass_sem.at[0]).wait())
    massbuf[0] = massown[0]

    pass_on(3)
    unit(0)
    for wait in sent:
        wait()
    pltpu.make_async_copy(others, others, mass_sem.at[1]).wait()
    mass = jnp.sum(massbuf[...], axis=0)
    inv = 1.0 / jnp.broadcast_to(mass, (BLK, LANES)).T
    mate_copy(0).wait_recv()
    total = fkeep[0] + fmate[0]
    for dy in (1, 2, 3):
        out_copy(dy).wait_recv()
        total = total + frecv[dy - 1].astype(jnp.float32)
    for k in range(feat.shape[1] // LANES):
        out[:, k * LANES:(k + 1) * LANES] = total[:, k * LANES:(k + 1) * LANES] * inv
    for dy in range(NY):
        mate_copy(dy).wait_send()
        if dy:
            out_copy(dy).wait_send()


def local(vehicle_emb, request_emb, request_feat, log_supply, log_demand):
    rows, cols, width = BLK * NB, request_emb.shape[0], request_feat.shape[1]
    cw = cols // NCHUNK
    f32, bf16 = jnp.float32, jnp.bfloat16
    dma = pltpu.SemaphoreType.DMA
    scratch = [
        pltpu.VMEM((NB, BLK, vehicle_emb.shape[1]), bf16),
        pltpu.VMEM(request_emb.shape, bf16),
        pltpu.VMEM(request_feat.shape, bf16),
        pltpu.VMEM((NB, 1, LANES), f32),
        pltpu.VMEM((1, cols), f32),
        pltpu.VMEM((rows, cols), f32),
        pltpu.VMEM((rows, cols), f32),
        pltpu.VMEM((8, cols), f32),
        pltpu.VMEM((8, cols), f32),
        pltpu.VMEM((1, cols), f32),
        pltpu.VMEM((1, cols), f32),
        pltpu.VMEM((NCHUNK, rows, LANES), f32),
        pltpu.VMEM((NCHUNK, rows, LANES), f32),
        pltpu.VMEM((NCHUNK, rows, LANES), f32),
        pltpu.VMEM((rows, LANES), f32),
        pltpu.VMEM((2, NCHUNK, NX, 1, cw), f32),
        pltpu.VMEM((2, NCHUNK, NZ, 1, cw), f32),
        pltpu.VMEM((NB, NB, 1, LANES), f32),
        pltpu.VMEM((NB, 1, LANES), f32),
        pltpu.VMEM((NB, 1, LANES), f32),
        pltpu.VMEM((NB, 1, LANES), f32),
        pltpu.VMEM((NY, BLK, width), f32),
        pltpu.VMEM((NY, BLK, width), f32),
        pltpu.VMEM((NY, BLK, width), f32),
        pltpu.VMEM((NY - 1, BLK, width), bf16),
        pltpu.VMEM((NY - 1, BLK, width), bf16),
        dma((4 + NCHUNK,)), dma((NB,)), dma((NB,)), pltpu.SemaphoreType.REGULAR((3,)),
        dma((2, NCHUNK)), dma((2, NCHUNK)), dma((2, NCHUNK)), dma((2, NCHUNK)),
        dma((2,)), dma((2,)),
        dma((NY,)), dma((NY,)), dma((NY - 1,)), dma((NY - 1,)),
    ]
    return pl.pallas_call(
        kernel,
        out_shape=pltpu.VMEM((BLK, width), f32),
        in_specs=[pl.BlockSpec(memory_space=pltpu.HBM)] * 5,
        out_specs=pl.BlockSpec(memory_space=pltpu.VMEM),
        scratch_shapes=scratch,
        compiler_params=pltpu.CompilerParams(
            collective_id=0, has_side_effects=True, vmem_limit_bytes=56 * 2**20),
        cost_estimate=pl.CostEstimate(
            flops=2 * rows * cols * (vehicle_emb.shape[1] + width), bytes_accessed=4 * 2**20,
            transcendentals=2 * rows * cols),
        name="sinkhorn_assign",
    )(vehicle_emb, request_emb, request_feat, log_supply.reshape(NB, 1, LANES), log_demand.reshape(1, cols))


def solution(mesh):
    in_specs = (P(("veh", "req"), None), P("req", None), P("req", None), P("veh"), P("req"))
    out_specs = P(("veh", "req"), None)
    return jax.shard_map(local, mesh=mesh, in_specs=in_specs, out_specs=out_specs, check_vma=False)
```
